256 devices in a mesh: dp: 64 (over x, z, core), ctx: 4 (over y).
Axes of the slice: x: 4, y: 4, z: 8, core: 2. Of those that a mesh axis runs over, the one named last changes fastest.
Arguments:
- queries: bfloat16 [32768, 2048], P(('dp', 'ctx')), may hold values from -100 to 100
- key_rows: bfloat16 [32768, 1024], P(('dp', 'ctx')), may hold values from -6 to 6
- values: bfloat16 [32768, 1024], P(('dp', 'ctx')), may hold values from -6 to 6
- saved_out: bfloat16 [32768, 2048], P(('dp', 'ctx')), may hold values from -6 to 6
- out_grad: bfloat16 [32768, 2048], P(('dp', 'ctx')), may hold values from -6 to 6
- pack_of: int32 [32768, 1], P(('dp', 'ctx')), may hold values from 0 to 63; in each aligned block of 128 rows (0 to 127, 128 to 255, ...) at most 3 rows name the same one
- segment_label: int32 [32768], P(('dp', 'ctx')), may hold values from 0 to 3
Outputs:
- grad_queries: bfloat16 [32768, 2048], P(('dp', 'ctx'))
- grad_keys: bfloat16 [32768, 1024], P(('dp', 'ctx'))
- grad_values: bfloat16 [32768, 1024], P(('dp', 'ctx'))
The draws below stay inside these ranges and needn't reach their ends.
Inputs may be any that keep to these rules, and one draw needn't show every extreme that they name: `pack_of`: the 128 rows of one device name each pack at most 3 times, a bound that some block reaches.
All inputs are finite; a program needn't handle non-finite values.
Results may differ from the reference program's by a relative error of at most 0.013.
Values may be sent and summed in bfloat16 or wider, within the bound.
A program may use at most 64 MiB of HBM per device.

```python
import functools
import math
import jax
import jax.numpy as jnp
import numpy as np
from jax import lax

HQ = 8
HK = 4
HD = 256
SEGS = 4
TOK_DEV = 128
CAP = 3
SLOTS = 192
TOKENS = 32768
N_DP = 64
N_CTX = 4


def shared_keys(key):
    return jax.random.truncated_normal(key, -6.0, 6.0, (TOKENS, HK * HD), jnp.float32)


def draw_key_rows(key, part):
    common = shared_keys(key)
    return common.astype(jnp.bfloat16)


def draw_queries(key, part):
    key = jax.random.fold_in(key, 9)
    fresh = jax.random.truncated_normal(key, -6.0, 6.0, (TOKENS, HQ * HD), jnp.float32)
    return fresh.astype(jnp.bfloat16)


def place_ends(drawn, stream_key, smallest, largest):
    dims = drawn.shape
    place = [jax.random.randint(jax.random.fold_in(stream_key, axis), (), 0, dims[axis]) for axis in range(len(dims))]
    drawn = drawn.at[tuple(place)].set(smallest)
    longest = dims.index(max(dims))
    place[longest] = (place[longest] + 1) % dims[longest]
    return drawn.at[tuple(place)].set(largest)


def block_levels(stream_key, extent, split, low, largest):
    level = 1.0
    for dim, parts in split:
        steps = jax.random.uniform(jax.random.fold_in(jax.random.fold_in(stream_key, 6), dim), (parts,), jnp.float32, low / len(split), largest / len(split))
        level = level * jnp.repeat(jnp.exp(steps), extent[dim] // parts).reshape((-1,) + (1,) * (len(extent) - 1 - dim))
    return level


def assign_block(key, own, number, rows, amount, top, limit, skew):
    sequence = jax.random.permutation(key, amount)
    heavy_load, usual = load_shares(amount, rows * top, limit, skew, True), load_shares(amount, rows * top, limit, skew, False)
    places = jnp.arange(amount)

    def named(lengths, turn):
        used = int((lengths > 0).sum())
        fixed = max(1, used // 4)
        passed = fixed + (places - fixed + turn * (used - fixed)) % max(1, amount - fixed)
        return jnp.zeros((amount,), jnp.int32).at[sequence[jnp.where(places < fixed, places, passed)]].set(jnp.asarray(lengths, jnp.int32))

    lengths = jnp.where(number % 4 == 0, named(heavy_load, number // 4), named(usual, number - number // 4 - 1))
    mixed = jax.random.permutation(jax.random.fold_in(own, 3), amount)
    giver, sink = mixed[0:amount // 2 * 2:2], mixed[1:amount // 2 * 2:2]
    slack = jnp.minimum(lengths[giver] - 1, limit - lengths[sink]) // 2
    slack = jnp.where((giver == sequence[0]) | (sink == sequence[0]) | (lengths[sink] == 0), 0, jnp.maximum(slack, 0))
    passed = jax.random.randint(jax.random.fold_in(own, 4), (amount // 2,), 0, 1 << 20) % (slack + 1)
    lengths = lengths.at[giver].add(-passed).at[sink].add(passed)
    members = jnp.searchsorted(jnp.cumsum(lengths), jnp.arange(rows * top), side="right").astype(jnp.int32)
    listing = members.reshape(top, rows).T
    listing = listing[jax.random.permutation(jax.random.fold_in(own, 1), rows)]
    turn = jax.random.randint(jax.random.fold_in(own, 2), (rows, 1), 0, top)
    return jnp.take_along_axis(listing, (jnp.arange(top)[None, :] + turn) % top, axis=1)


def load_shares(number_of, total, limit, slope, full):
    loads = [(1 << 20) // math.isqrt(rank ** slope) + 1 for rank in range(1, number_of + 1)]
    largest = limit if full else min(limit, max(-(-total // number_of), total * loads[0] // sum(loads)))
    least = 1 if total - largest >= number_of - 1 else 0
    holding, rest = [largest] + [least] * (number_of - 1), total - largest - least * (number_of - 1)
    while rest > 0:
        free = [i for i in range(1, number_of) if holding[i] < largest] or [i for i in range(1, number_of) if holding[i] < limit]
        mass, left = sum([loads[i] for i in free]), rest
        for i in free:
            more = min(limit - holding[i], max(1, left * loads[i] // mass), rest)
            holding[i] = holding[i] + more
            rest = rest - more
    return np.array(holding)


def gaussian(stream_key, shape, scale, most, split=(), kind=jnp.bfloat16):
    values = scale * jax.random.normal(stream_key, shape, jnp.float32)
    if split:
        values = values * block_levels(stream_key, shape, split, -0.22, 0.18)
    return jnp.clip(values, -most, most).astype(kind)


def setup_inputs(seed: int = 0) -> dict:
    key_of = jax.random.split(jax.random.key(seed), 8)
    queries = draw_queries(jax.random.fold_in(key_of[7], 71), 0)
    key_rows = draw_key_rows(jax.random.fold_in(key_of[7], 71), 0)
    values = gaussian(key_of[2], (TOKENS, HK * HD), 1.0, 6.0, ((0, 256),))
    saved_out = gaussian(key_of[3], (TOKENS, HQ * HD), 1.0, 6.0, ((0, 256),))
    out_grad = gaussian(key_of[4], (TOKENS, HQ * HD), 1.0, 6.0, ((0, 256),))
    pack_of_keys = jax.random.split(jax.random.fold_in(key_of[5], 1), TOKENS // TOK_DEV)
    pack_of_turns = jax.random.permutation(jax.random.fold_in(key_of[5], 3), TOKENS // TOK_DEV)
    pack_of = jax.vmap(lambda own, number: assign_block(jax.random.fold_in(key_of[5], 2), own, number, TOK_DEV, N_DP, 1, CAP, 2))(pack_of_keys, pack_of_turns).reshape((TOKENS, 1))
    segment_label = place_ends(jax.random.randint(key_of[6], (TOKENS,), 0, SEGS), jax.random.fold_in(key_of[6], 1), 0, SEGS - 1).astype(jnp.int32)
    return dict(queries=queries, key_rows=key_rows, values=values, saved_out=saved_out, out_grad=out_grad, pack_of=pack_of, segment_label=segment_label)


MASKED = -1e+30

def device_ranks(target, dest_count):
    onehot = (target[:, None] == jnp.arange(dest_count, dtype=jnp.int32)[None, :]).astype(jnp.int32)
    before = jnp.cumsum(onehot, axis=0) - onehot
    return lax.optimization_barrier(jnp.sum(before * onehot, axis=1)).astype(jnp.int32)

def row_products(grad_rows, out_rows):
    product = grad_rows.astype(jnp.float32) * out_rows.astype(jnp.float32)
    return lax.optimization_barrier(jnp.sum(product.reshape(product.shape[0], HQ, HD), axis=2)).astype(jnp.bfloat16)

def attend_exact(query_rows, grad_rows, delta_rows, query_label, key_head, value_head, key_label, score_scale):
    scores = jnp.einsum('rgd,kd->grk', query_rows, key_head) * score_scale
    allowed = (query_label[:, None] == key_label[None, :]) & (key_label[None, :] > 0.5)
    scores = jnp.where(allowed[None], scores, MASKED)
    row_max = lax.optimization_barrier(jnp.max(scores, axis=2, keepdims=True))
    logsum = row_max + jnp.log(lax.optimization_barrier(jnp.sum(jnp.exp(scores - row_max), axis=2, keepdims=True)))
    probs_full = jnp.exp(scores - logsum)
    dprobs = jnp.einsum('rgd,kd->grk', grad_rows, value_head)
    offset = jnp.transpose(delta_rows.astype(jnp.float32))[:, :, None]
    dscore = (probs_full * (dprobs - offset) * score_scale).astype(jnp.bfloat16)
    return (probs_full.astype(jnp.bfloat16), dscore)

def reference(queries, key_rows, values, saved_out, out_grad, pack_of, segment_label):
    capacity = CAP
    slots = SLOTS
    group_size = HQ // HK
    score_scale = 1.0 / math.sqrt(HD)
    pack_rows = N_CTX * slots
    target = pack_of[:, 0].astype(jnp.int32)
    ranker = functools.partial(device_ranks, dest_count=N_DP)
    ranks = jax.vmap(ranker)(target.reshape(N_DP * N_CTX, TOK_DEV)).reshape(TOKENS)
    device = jnp.arange(TOKENS, dtype=jnp.int32) // TOK_DEV
    position = ((target * N_CTX + device % N_CTX) * slots + device // N_CTX * capacity + ranks).astype(jnp.int32)
    whole = N_DP * pack_rows

    def to_slots(matrix):
        return jnp.zeros((whole,) + matrix.shape[1:], matrix.dtype).at[position].set(matrix)
    row_delta = row_products(out_grad, saved_out)
    labels = (segment_label + 1).astype(jnp.float32)
    packed = (to_slots(queries), to_slots(key_rows), to_slots(values), to_slots(out_grad), to_slots(row_delta), to_slots(labels))
    packed = tuple((piece.reshape((N_DP, pack_rows) + piece.shape[1:]) for piece in packed))

    def one_pack(pieces):
        pack_q, pack_k, pack_v, pack_g, pack_d, pack_l = pieces
        q_heads = []
        k_heads = []
        v_heads = []
        for head in range(HK):
            qcols = slice(head * group_size * HD, (head + 1) * group_size * HD)
            kcols = slice(head * HD, (head + 1) * HD)
            key_head = pack_k[:, kcols].astype(jnp.float32)
            value_head = pack_v[:, kcols].astype(jnp.float32)
            key_sum = jnp.zeros((pack_rows, HD), jnp.float32)
            value_sum = jnp.zeros((pack_rows, HD), jnp.float32)
            grad_blocks = []
            for block in range(N_CTX):
                brows = slice(block * slots, (block + 1) * slots)
                query_rows = pack_q[brows, qcols].reshape(slots, group_size, HD).astype(jnp.float32)
                grad_rows = pack_g[brows, qcols].reshape(slots, group_size, HD).astype(jnp.float32)
                delta_rows = pack_d[brows, head * group_size:(head + 1) * group_size]
                weights, dscore = attend_exact(query_rows, grad_rows, delta_rows, pack_l[brows], key_head, value_head, pack_l, score_scale)
                dscore_wide = dscore.astype(jnp.float32)
                grad_blocks.append(jnp.einsum('grk,kd->rgd', dscore_wide, key_head).reshape(slots, group_size * HD))
                key_part = jnp.einsum('grk,rgd->kd', dscore_wide, query_rows).astype(jnp.bfloat16)
                value_part = jnp.einsum('grk,rgd->kd', weights.astype(jnp.float32), grad_rows).astype(jnp.bfloat16)
                key_sum = key_sum + lax.optimization_barrier(key_part).astype(jnp.float32)
                value_sum = value_sum + lax.optimization_barrier(value_part).astype(jnp.float32)
            q_heads.append(jnp.concatenate(grad_blocks, axis=0))
            k_heads.append(key_sum)
            v_heads.append(value_sum)
        grad_q = jnp.concatenate(q_heads, axis=1).astype(jnp.bfloat16)
        grad_k = jnp.concatenate(k_heads, axis=1).astype(jnp.bfloat16)
        grad_v = jnp.concatenate(v_heads, axis=1).astype(jnp.bfloat16)
        return (grad_q, grad_k, grad_v)
    grad_q, grad_k, grad_v = lax.map(one_pack, packed)
    grad_queries = grad_q.reshape(whole, HQ * HD)[position]
    grad_keys = grad_k.reshape(whole, HK * HD)[position]
    grad_values = grad_v.reshape(whole, HK * HD)[position]
    return (grad_queries, grad_keys, grad_values)
```

```python
import jax
import jax.numpy as jnp
from jax import lax
from jax.experimental import pallas as pl
from jax.experimental.pallas import tpu as pltpu
from jax.sharding import PartitionSpec as P

MESH = pl.DeviceIdType.MESH
F32 = jnp.float32
BF16 = jnp.bfloat16

NDP = 64
NY = 4
TOK = 128
CAP = 3
HD = 256
SLOT = NY * CAP
ROWS = NDP * SLOT
GRP = 8
MASKED = -1e30
SCALE = 1.0 / 16.0

NT, NB = 6, 4


def iota(shape, dim):
    return lax.broadcasted_iota(jnp.int32, shape, dim)


def mm(a, b, ca, cb):
    return lax.dot_general(a, b, (((ca,), (cb,)), ((), ())), preferred_element_type=F32)


def partner(i, x, z, c):
    nx = lax.rem(x + i // 16, 4)
    nz = lax.rem(z + lax.rem(i // 2, 8), 8)
    nc = lax.rem(c + i, 2)
    return (nx * 8 + nz) * 2 + nc


def kernel(
    q_ref, k_ref, v_ref, g_ref, o_ref, pcol_ref, prow_ref, lab_ref,
    oq_ref, ok_ref, ov_ref,
    tok, meta_s, meta_r, place, gather, fsend, frecv, msend, mrecv, xs, rowv, labk,
    dq_acc, dk_acc, dv_acc, bsend, brecv, obuf,
    ysend, yrecv, ymsend, ymrecv, zsend, zrecv, zmsend, zmrecv, bsem_s, bsem_r, osem_s, osem_r,
):
    dp = lax.axis_index("dp")
    y = lax.axis_index("ctx")
    x, z, c = dp // 16, lax.rem(dp // 2, 8), lax.rem(dp, 2)
    bar = pltpu.get_barrier_semaphore()

    def greet(i, carry):
        pl.semaphore_signal(bar, inc=1, device_id=(partner(i, x, z, c), y), device_id_type=MESH)
        return carry

    lax.fori_loop(1, NDP, greet, 0)
    for dy in range(1, NY):
        pl.semaphore_signal(bar, inc=1, device_id=(dp, lax.rem(y + dy, NY)), device_id_type=MESH)

    pcol = pcol_ref[...]
    prow = prow_ref[...]
    earlier = (pcol == prow) & (iota((TOK, TOK), 0) < iota((TOK, TOK), 1))
    rank = jnp.sum(earlier.astype(F32), axis=0, keepdims=True)
    slot = rank + (y * CAP).astype(F32)
    lab = lab_ref[...].astype(F32) + 1.0

    prod = g_ref[...].astype(F32) * o_ref[...].astype(F32)
    hi = prod.astype(BF16)
    lo = (prod - hi.astype(F32)).astype(BF16)
    pick = (iota((8, 8 * HD), 1) // HD == iota((8, 8 * HD), 0)).astype(BF16)
    delta = (mm(pick, hi, 1, 1) + mm(pick, lo, 1, 1)).astype(BF16).astype(F32)
    for t in range(NY):
        meta_s[t, 0:1, :] = prow.astype(F32)
        meta_s[t, 1:2, :] = slot
        meta_s[t, 2:3, :] = lab
        meta_s[t, 3:5, :] = delta[2 * t : 2 * t + 2, :]
        meta_s[t, 5:8, :] = jnp.zeros((3, TOK), F32)
    meta_r[y] = meta_s[y]

    pl.semaphore_wait(bar, NDP - 1 + NY - 1)

    def columns(kind, head):
        if kind == 0:
            return k_ref.at[:, pl.ds(pl.multiple_of(head * HD, HD), HD)]
        if kind == 1:
            return v_ref.at[:, pl.ds(pl.multiple_of(head * HD, HD), HD)]
        ref = q_ref if kind % 2 == 0 else g_ref
        return ref.at[:, pl.ds(pl.multiple_of(head * 2 * HD + (kind // 2 - 1) * HD, HD), HD)]

    for dy in range(1, NY):
        t = lax.rem(y + dy, NY)
        pltpu.make_async_remote_copy(
            src_ref=meta_s.at[t], dst_ref=meta_r.at[y], send_sem=ymsend, recv_sem=ymrecv,
            device_id=(dp, t), device_id_type=MESH,
        ).start()
    for kind in range(NT):
        for dy in range(1, NY):
            t = lax.rem(y + dy, NY)
            pltpu.make_async_remote_copy(
                src_ref=columns(kind, t), dst_ref=tok.at[kind, y], send_sem=ysend, recv_sem=yrecv.at[kind // 2],
                device_id=(dp, t), device_id_type=MESH,
            ).start()
        pltpu.make_async_copy(columns(kind, y), tok.at[kind, y], yrecv.at[kind // 2]).start()

    pltpu.make_async_copy(meta_s.at[pl.ds(0, NY - 1)], meta_r.at[pl.ds(0, NY - 1)], ymrecv).wait()
    packs = jnp.concatenate([meta_r[t, 0:1, :] for t in range(NY)], axis=1)
    slots = jnp.concatenate([meta_r[t, 1:2, :] for t in range(NY)], axis=1)
    where = (packs * (2.0 * SLOT) + slots).astype(jnp.int32)

    def place_block(b, carry):
        r = iota((HD, NY * TOK), 0) + b * HD
        at = pl.ds(pl.multiple_of(b * HD, HD), HD)
        place[at, 0 : NY * TOK] = (r == where).astype(F32).astype(BF16)
        place[at, NY * TOK : 2 * NY * TOK] = (r == where + SLOT).astype(F32).astype(BF16)
        return carry

    lax.fori_loop(0, 2 * ROWS // HD, place_block, 0)

    owner = (iota((NDP, NY * TOK), 0).astype(F32) == packs).astype(F32).astype(BF16)
    lane = iota((128, NY * TOK), 0)
    vals = [jnp.concatenate([meta_r[t, 2 + j : 3 + j, :] for t in range(NY)], axis=1) for j in range(3)]
    kindv = jnp.where(lane // 16 == 0, vals[0], jnp.where(lane // 16 == 1, vals[1], vals[2]))
    hit = (lax.rem(lane, 16).astype(F32) == slots) & (lane < 48)
    small = jnp.where(hit, kindv, 0.0).astype(BF16)
    msend[...] = mm(owner, small, 1, 1).reshape(NDP, 1, 128)

    def meta_out(i, carry):
        d = partner(i, x, z, c)
        pltpu.make_async_remote_copy(
            src_ref=msend.at[d], dst_ref=mrecv.at[dp], send_sem=zmsend, recv_sem=zmrecv,
            device_id=(d, y), device_id_type=MESH,
        ).start()
        return carry

    for chunk in range(3):
        both = pl.ds(2 * chunk, 2)
        pltpu.make_async_copy(tok.at[both], tok.at[both], yrecv.at[chunk]).wait()
        for j in range(2):
            t = tok[2 * chunk + j].reshape(NY * TOK, HD)
            halves = jnp.concatenate([t[:, 0:128], t[:, 128:256]], axis=0)

            def fill(b, carry):
                got = mm(place[pl.ds(pl.multiple_of(b * 192, 192), 192), :], halves, 1, 0)
                fsend[chunk, pl.ds(b * GRP, GRP), 3 * j : 3 * j + 3] = got.astype(BF16).reshape(GRP, 3, 8, 128)
                return carry

            lax.fori_loop(0, NDP // GRP, fill, 0)

        def out(i, carry):
            d = partner(i, x, z, c)
            pltpu.make_async_remote_copy(
                src_ref=fsend.at[chunk, d], dst_ref=frecv.at[chunk, dp], send_sem=zsend, recv_sem=zrecv.at[chunk],
                device_id=(d, y), device_id_type=MESH,
            ).start()
            return carry

        lax.fori_loop(1, NDP, out, 0)
        pltpu.make_async_copy(fsend.at[chunk, dp], frecv.at[chunk, dp], zrecv.at[chunk]).start()
        if chunk == 0:
            lax.fori_loop(1, NDP, meta_out, 0)
            pltpu.make_async_copy(msend.at[dp], mrecv.at[dp], zmrecv).start()

    eye = (iota((TOK, TOK), 0) == iota((TOK, TOK), 1)).astype(F32).astype(BF16)
    for t in range(NY):
        col = mm(eye, meta_r[t].astype(BF16), 1, 1)
        home = (col[:, 0:1] * (2.0 * SLOT) + col[:, 1:2]).astype(jnp.int32)
        for half in range(2):
            row = half * NY * TOK + t * TOK

            def gather_block(b, carry):
                r = iota((TOK, HD), 1) + b * HD
                gather[row : row + TOK, pl.ds(pl.multiple_of(b * HD, HD), HD)] = (
                    (r == home + half * SLOT).astype(F32).astype(BF16)
                )
                return carry

            lax.fori_loop(0, 2 * ROWS // HD, gather_block, 0)

    a, b = iota((192, 192), 0), iota((192, 192), 1)
    split = (b == (lax.rem(a, 96) // 12) * 24 + (a // 96) * 12 + lax.rem(a, 12)).astype(F32).astype(BF16)
    join = (a == (lax.rem(b, 96) // 12) * 24 + (b // 96) * 12 + lax.rem(b, 12)).astype(F32).astype(BF16)

    pltpu.make_async_copy(mrecv, mrecv, zmrecv).wait()
    spread = (iota((ROWS, NDP), 0) // SLOT == iota((ROWS, NDP), 1)).astype(F32).astype(BF16)
    rows = mm(spread, mrecv[...].reshape(NDP, 128).astype(BF16), 1, 0)
    r12, l128 = lax.rem(iota((ROWS, 128), 0), SLOT), iota((ROWS, 128), 1)
    own = jnp.where((lax.rem(l128, 16) == r12) & (l128 < 48), rows, 0.0)
    labcol = jnp.sum(jnp.where(l128 < 16, own, 0.0), axis=1, keepdims=True)
    labk[...] = jnp.broadcast_to(jnp.where(labcol > 0.5, labcol, -1.0), (ROWS, 128))
    pick16 = (iota((8, 128), 1) // 16 == iota((8, 128), 0)).astype(F32).astype(BF16)
    rowv[...] = mm(pick16, own.astype(BF16), 1, 1)

    def take(chunk):
        pltpu.make_async_copy(frecv.at[chunk], frecv.at[chunk], zrecv.at[chunk]).wait()

        def unmix(b, carry):
            for j in range(2):
                block = frecv[chunk, pl.ds(b * GRP, GRP), 3 * j : 3 * j + 3].reshape(192, 128)
                got = mm(split, block, 1, 0).astype(BF16)
                at = pl.ds(pl.multiple_of(b * 96, 96), 96)
                xs[2 * chunk + j, at, 0:128] = got[0:96]
                xs[2 * chunk + j, at, 128:256] = got[96:192]
            return carry

        lax.fori_loop(0, NDP // GRP, unmix, 0)

    def give(kind, value):
        def mix(b, carry):
            at = pl.ds(pl.multiple_of(b * 96, 96), 96)
            v = value[at, :].astype(BF16)
            block = jnp.concatenate([v[:, 0:128], v[:, 128:256]], axis=0)
            got = mm(join, block, 1, 0).astype(BF16)
            bsend[kind, pl.ds(b * GRP, GRP)] = got.reshape(GRP, 3, 8, 128)
            return carry

        lax.fori_loop(0, NDP // GRP, mix, 0)

    def back(kind):
        def send(i, carry):
            d = partner(i, x, z, c)
            pltpu.make_async_remote_copy(
                src_ref=bsend.at[kind, d], dst_ref=brecv.at[kind, dp], send_sem=bsem_s, recv_sem=bsem_r.at[kind],
                device_id=(d, y), device_id_type=MESH,
            ).start()
            return carry

        lax.fori_loop(1, NDP, send, 0)
        pltpu.make_async_copy(bsend.at[kind, dp], brecv.at[kind, dp], bsem_r.at[kind]).start()

    take(0)
    for g in range(2):
        take(1 + g)
        if g == 1:
            back(0)

        def attend(b, carry):
            at = pl.ds(pl.multiple_of(b * HD, HD), HD)
            key, val = xs[0], xs[1]
            qb, gb = xs[2 + 2 * g, at, :], xs[3 + 2 * g, at, :]
            s = mm(key, qb, 1, 1) * SCALE
            ok = labk[:, 0:1] == rowv[0:1, at]
            s = jnp.where(ok, s, MASKED)
            top = jnp.max(s, axis=0, keepdims=True)
            e = jnp.exp(s - top)
            p = e * (1.0 / jnp.sum(e, axis=0, keepdims=True))
            d = mm(val, gb, 1, 1) - rowv[1 + g : 2 + g, at]
            ds = (p * d).astype(BF16)
            pv = mm(p.astype(BF16), gb, 1, 0)
            pk = mm(ds, qb, 1, 0)
            if g == 0:
                first = b == 0
                dv_acc[...] = jnp.where(first, 0.0, dv_acc[...]) + pv
                dk_acc[...] = jnp.where(first, 0.0, dk_acc[...]) + pk
            else:
                dv_acc[...] += pv
                dk_acc[...] += pk
            dq_acc[at, :] = mm(ds, key, 0, 0) * SCALE
            return carry

        if g == 0:
            dv_acc[...] = jnp.zeros((ROWS, HD), F32)
            dk_acc[...] = jnp.zeros((ROWS, HD), F32)
        lax.fori_loop(0, ROWS // HD, attend, 0)
        give(g, dq_acc)
    back(1)
    dk_acc[...] = dk_acc[...] * SCALE
    give(2, dk_acc)
    back(2)
    give(3, dv_acc)
    back(3)

    for kind in range(NB):
        pltpu.make_async_copy(brecv.at[kind], brecv.at[kind], bsem_r.at[kind]).wait()
        got = mm(gather[...], brecv[kind].reshape(2 * ROWS, 128), 1, 0).astype(BF16)
        for t in range(NY):
            obuf[kind, t, :, 0:128] = got[t * TOK : (t + 1) * TOK]
            obuf[kind, t, :, 128:256] = got[(NY + t) * TOK : (NY + t + 1) * TOK]
        ref = (oq_ref, oq_ref, ok_ref, ov_ref)[kind]
        if kind < 2:
            cols = pl.ds(pl.multiple_of(y * 2 * HD + kind * HD, HD), HD)
        else:
            cols = pl.ds(pl.multiple_of(y * HD, HD), HD)
        for dy in range(1, NY):
            t = lax.rem(y + dy, NY)
            pltpu.make_async_remote_copy(
                src_ref=obuf.at[kind, t], dst_ref=ref.at[:, cols], send_sem=osem_s, recv_sem=osem_r.at[max(0, kind - 1)],
                device_id=(dp, t), device_id_type=MESH,
            ).start()
        pltpu.make_async_copy(obuf.at[kind, y], ref.at[:, cols], osem_r.at[max(0, kind - 1)]).start()

    pltpu.make_async_copy(oq_ref, oq_ref, osem_r.at[0]).wait()
    pltpu.make_async_copy(ok_ref, ok_ref, osem_r.at[1]).wait()
    pltpu.make_async_copy(ov_ref, ov_ref, osem_r.at[2]).wait()
    some = pl.ds(0, NY - 1)
    pltpu.make_async_copy(meta_s.at[some], meta_s.at[some], ymsend).wait()
    pltpu.make_async_copy(tok.at[:, some], tok.at[:, some], ysend).wait()
    pltpu.make_async_copy(obuf.at[:, some], obuf.at[:, some], osem_s).wait()
    most = pl.ds(0, NDP - 1)
    pltpu.make_async_copy(msend.at[most], msend.at[most], zmsend).wait()
    pltpu.make_async_copy(fsend.at[:, most], fsend.at[:, most], zsend).wait()
    pltpu.make_async_copy(bsend.at[:, most], bsend.at[:, most], bsem_s).wait()


def body(queries, key_rows, values, saved_out, out_grad, pack_of, segment_label):
    anywhere = pl.BlockSpec(memory_space=pl.ANY)
    vmem = pl.BlockSpec(memory_space=pltpu.VMEM)
    dma = pltpu.SemaphoreType.DMA
    return pl.pallas_call(
        kernel,
        out_shape=(
            jax.ShapeDtypeStruct((TOK, 8 * HD), BF16),
            jax.ShapeDtypeStruct((TOK, 4 * HD), BF16),
            jax.ShapeDtypeStruct((TOK, 4 * HD), BF16),
        ),
        in_specs=[anywhere] * 3 + [vmem] * 5,
        out_specs=(anywhere,) * 3,
        scratch_shapes=[
            pltpu.VMEM((NT, NY, TOK, HD), BF16),
            pltpu.VMEM((NY, 8, TOK), F32),
            pltpu.VMEM((NY, 8, TOK), F32),
            pltpu.VMEM((2 * ROWS, 2 * NY * TOK), BF16),
            pltpu.VMEM((2 * NY * TOK, 2 * ROWS), BF16),
            pltpu.VMEM((3, NDP, 6, 8, 128), BF16),
            pltpu.VMEM((3, NDP, 6, 8, 128), BF16),
            pltpu.VMEM((NDP, 1, 128), F32),
            pltpu.VMEM((NDP, 1, 128), F32),
            pltpu.VMEM((NT, ROWS, HD), BF16),
            pltpu.VMEM((8, ROWS), F32),
            pltpu.VMEM((ROWS, 128), F32),
            pltpu.VMEM((ROWS, HD), F32),
            pltpu.VMEM((ROWS, HD), F32),
            pltpu.VMEM((ROWS, HD), F32),
            pltpu.VMEM((NB, NDP, 3, 8, 128), BF16),
            pltpu.VMEM((NB, NDP, 3, 8, 128), BF16),
            pltpu.VMEM((NB, NY, TOK, HD), BF16),
            dma, dma((3,)), dma, dma, dma, dma((3,)), dma, dma, dma, dma((NB,)), dma, dma((3,)),
        ],
        compiler_params=pltpu.CompilerParams(
            collective_id=0, has_side_effects=True, vmem_limit_bytes=52 << 20
        ),
        name="packed_attention_backward",
    )(
        queries, key_rows, values, out_grad, saved_out,
        pack_of, pack_of.reshape(1, TOK), segment_label.reshape(1, TOK),
    )


def solution(mesh):
    rows = P(("dp", "ctx"), None)
    return jax.shard_map(
        body,
        mesh=mesh,
        in_specs=(rows, rows, rows, rows, rows, rows, P(("dp", "ctx"))),
        out_specs=(rows, rows, rows),
        check_vma=False,
    )
```

```python
import jax
import jax.numpy as jnp
from jax import lax
from jax.experimental import pallas as pl
from jax.experimental.pallas import tpu as pltpu
from jax.sharding import PartitionSpec as P

MESH = pl.DeviceIdType.MESH
F32 = jnp.float32
BF16 = jnp.bfloat16

NDP = 64
NY = 4
TOK = 128
CAP = 3
HD = 256
SLOT = NY * CAP
ROWS = NDP * SLOT
GRP = 8
MASKED = -1e30
SCALE = 1.0 / 16.0

NT, NB = 6, 4


def iota(shape, dim):
    return lax.broadcasted_iota(jnp.int32, shape, dim)


def mm(a, b, ca, cb):
    return lax.dot_general(a, b, (((ca,), (cb,)), ((), ())), preferred_element_type=F32)


def kernel(
    q_ref, k_ref, v_ref, g_ref, o_ref, pack_ref, lab_ref,
    oq_ref, ok_ref, ov_ref,
    ints, gv, ov, tok, meta_s, meta_r, del_s, del_r, place, gather, fsend, frecv, msend, mrecv, xs, rowv, labk,
    dq_acc, dk_acc, dv_acc, bsend, brecv, obuf,
    insem, isem, ysend, yrecv, ymsend, ymrecv, ydsend, ydrecv, zsend, zrecv, zmsend, zmrecv,
    bsem_s, bsem_r, osem_s, osem_r, plane_sem, core_sem,
):
    dp = lax.axis_index("dp")
    y = lax.axis_index("ctx")
    x, z, c = dp // 16, lax.rem(dp // 2, 8), lax.rem(dp, 2)
    bar = pltpu.get_barrier_semaphore()

    def at(nx, nz, nc):
        return (nx * 8 + nz) * 2 + nc

    def greet(sem, d, t):
        pl.semaphore_signal(sem, inc=1, device_id=(d, t), device_id_type=MESH)

    ring_x = [at(lax.rem(x + j, 4), z, c) for j in range(1, 4)]
    other = at(x, z, 1 - c)
    ring_y = [lax.rem(y + j, NY) for j in range(1, NY)]
    for t in ring_y:
        greet(bar, dp, t)
    for d in ring_x:
        greet(bar, d, y)
    greet(bar, other, y)
    for j in range(1, 8):
        greet(bar, at(x, lax.rem(z + j, 8), c), y)

    copies = [
        pltpu.make_async_copy(pack_ref, ints.at[0], isem.at[0]),
        pltpu.make_async_copy(lab_ref, ints.at[1], isem.at[1]),
        pltpu.make_async_copy(g_ref, gv, insem.at[0]),
        pltpu.make_async_copy(o_ref, ov, insem.at[1]),
    ]
    for copy in copies:
        copy.start()

    def columns(kind, head):
        if kind == 0:
            return k_ref.at[:, pl.ds(pl.multiple_of(head * HD, HD), HD)]
        if kind == 1:
            return v_ref.at[:, pl.ds(pl.multiple_of(head * HD, HD), HD)]
        ref = q_ref if kind % 2 == 0 else g_ref
        return ref.at[:, pl.ds(pl.multiple_of(head * 2 * HD + (kind // 2 - 1) * HD, HD), HD)]

    for kind in range(NT):
        pltpu.make_async_copy(columns(kind, y), tok.at[kind, y], yrecv.at[kind]).start()

    eye = (iota((TOK, TOK), 0) == iota((TOK, TOK), 1)).astype(F32).astype(BF16)
    copies[0].wait()
    copies[1].wait()
    prow = ints[0].astype(F32)
    pcol = mm(eye, jnp.broadcast_to(prow, (8, TOK)).astype(BF16), 1, 1)[:, 0:1]
    earlier = (pcol == prow) & (iota((TOK, TOK), 0) < iota((TOK, TOK), 1))
    rank = jnp.sum(earlier.astype(F32), axis=0, keepdims=True)
    slot = rank + (y * CAP).astype(F32)
    meta_s[0:1, :] = prow
    meta_s[1:2, :] = slot
    meta_s[2:3, :] = ints[1].astype(F32) + 1.0
    meta_s[3:8, :] = jnp.zeros((5, TOK), F32)
    meta_r[y] = meta_s[...]

    pl.semaphore_wait(bar, 14)

    for t in ring_y:
        pltpu.make_async_remote_copy(
            src_ref=meta_s, dst_ref=meta_r.at[y], send_sem=ymsend, recv_sem=ymrecv,
            device_id=(dp, t), device_id_type=MESH,
        ).start()
    for kind in range(NT):
        for t in ring_y:
            pltpu.make_async_remote_copy(
                src_ref=columns(kind, t), dst_ref=tok.at[kind, y], send_sem=ysend, recv_sem=yrecv.at[kind],
                device_id=(dp, t), device_id_type=MESH,
            ).start()

    for d in ring_x:
        greet(plane_sem, d, y)
    pl.semaphore_wait(plane_sem, 3)
    greet(core_sem, other, y)
    pl.semaphore_wait(core_sem, 1)

    pltpu.make_async_copy(meta_r.at[pl.ds(0, NY - 1)], meta_r.at[pl.ds(0, NY - 1)], ymrecv).wait()
    packs = jnp.concatenate([meta_r[t, 0:1, :] for t in range(NY)], axis=1)
    slots = jnp.concatenate([meta_r[t, 1:2, :] for t in range(NY)], axis=1)
    where = (packs * (2.0 * SLOT) + slots).astype(jnp.int32)

    def place_block(b, carry):
        r = iota((HD, NY * TOK), 0) + b * HD
        at = pl.ds(pl.multiple_of(b * HD, HD), HD)
        place[at, 0 : NY * TOK] = (r == where).astype(F32).astype(BF16)
        place[at, NY * TOK : 2 * NY * TOK] = (r == where + SLOT).astype(F32).astype(BF16)
        return carry

    lax.fori_loop(0, 2 * ROWS // HD, place_block, 0)

    base = dp // GRP
    spin = [lax.rem(dp + j, GRP) for j in range(GRP)]

    def spread_out(g, src, dst, ssem, rsem):
        for j in range(GRP):
            d = g * GRP + spin[j]

            @pl.when(d != dp)
            def _():
                pltpu.make_async_remote_copy(
                    src_ref=src.at[d], dst_ref=dst.at[dp], send_sem=ssem, recv_sem=rsem,
                    device_id=(d, y), device_id_type=MESH,
                ).start()

    def forward(kind):
        pltpu.make_async_copy(tok.at[kind], tok.at[kind], yrecv.at[kind]).wait()

        def fill(k, carry):
            g = lax.rem(base + k, GRP)
            t = tok[kind].reshape(NY * TOK, HD)
            halves = jnp.concatenate([t[:, 0:128], t[:, 128:256]], axis=0)
            got = mm(place[pl.ds(pl.multiple_of(g * 192, 192), 192), :], halves, 1, 0)
            fsend[kind, pl.ds(g * GRP, GRP)] = got.astype(BF16).reshape(GRP, 3, 8, 128)
            spread_out(g, fsend.at[kind], frecv.at[kind], zsend, zrecv.at[kind])
            return carry

        lax.fori_loop(1, GRP + 1, fill, 0)
        pltpu.make_async_copy(fsend.at[kind, dp], frecv.at[kind, dp], zrecv.at[kind]).start()

    for kind in range(NT):
        forward(kind)
        if kind == 0:
            copies[2].wait()
            copies[3].wait()
            prod = gv[...].astype(F32) * ov[...].astype(F32)
            hi = prod.astype(BF16)
            lo = (prod - hi.astype(F32)).astype(BF16)
            pick = (iota((8, 8 * HD), 1) // HD == iota((8, 8 * HD), 0)).astype(BF16)
            delta = (mm(pick, hi, 1, 1) + mm(pick, lo, 1, 1)).astype(BF16).astype(F32)
            for t in range(NY):
                del_s[t, 0:2, :] = delta[2 * t : 2 * t + 2, :]
                del_s[t, 2:8, :] = jnp.zeros((6, TOK), F32)
            del_r[y] = del_s[y]
            for t in ring_y:
                pltpu.make_async_remote_copy(
                    src_ref=del_s.at[t], dst_ref=del_r.at[y], send_sem=ydsend, recv_sem=ydrecv,
                    device_id=(dp, t), device_id_type=MESH,
                ).start()
        if kind == 1:
            pltpu.make_async_copy(del_r.at[pl.ds(0, NY - 1)], del_r.at[pl.ds(0, NY - 1)], ydrecv).wait()
            owner = (iota((NDP, NY * TOK), 0).astype(F32) == packs).astype(F32).astype(BF16)
            lane = iota((128, NY * TOK), 0)
            vals = [jnp.concatenate([meta_r[t, 2:3, :] for t in range(NY)], axis=1)]
            vals += [jnp.concatenate([del_r[t, j : j + 1, :] for t in range(NY)], axis=1) for j in range(2)]
            kindv = jnp.where(lane // 16 == 0, vals[0], jnp.where(lane // 16 == 1, vals[1], vals[2]))
            hit = (lax.rem(lane, 16).astype(F32) == slots) & (lane < 48)
            small = jnp.where(hit, kindv, 0.0).astype(BF16)
            msend[...] = mm(owner, small, 1, 1).reshape(NDP, 1, 128)

            def meta_out(k, carry):
                spread_out(lax.rem(base + k, GRP), msend, mrecv, zmsend, zmrecv)
                return carry

            lax.fori_loop(1, GRP + 1, meta_out, 0)
            pltpu.make_async_copy(msend.at[dp], mrecv.at[dp], zmrecv).start()

    for t in range(NY):
        col = mm(eye, meta_r[t].astype(BF16), 1, 1)
        home = (col[:, 0:1] * (2.0 * SLOT) + col[:, 1:2]).astype(jnp.int32)
        for half in range(2):
            row = half * NY * TOK + t * TOK

            def gather_block(b, carry):
                r = iota((TOK, HD), 1) + b * HD
                gather[row : row + TOK, pl.ds(pl.multiple_of(b * HD, HD), HD)] = (
                    (r == home + half * SLOT).astype(F32).astype(BF16)
                )
                return carry

            lax.fori_loop(0, 2 * ROWS // HD, gather_block, 0)

    a, b = iota((192, 192), 0), iota((192, 192), 1)
    split = (b == (lax.rem(a, 96) // 12) * 24 + (a // 96) * 12 + lax.rem(a, 12)).astype(F32).astype(BF16)
    join = (a == (lax.rem(b, 96) // 12) * 24 + (b // 96) * 12 + lax.rem(b, 12)).astype(F32).astype(BF16)

    pltpu.make_async_copy(mrecv, mrecv, zmrecv).wait()
    spread = (iota((ROWS, NDP), 0) // SLOT == iota((ROWS, NDP), 1)).astype(F32).astype(BF16)
    rows = mm(spread, mrecv[...].reshape(NDP, 128).astype(BF16), 1, 0)
    r12, l128 = lax.rem(iota((ROWS, 128), 0), SLOT), iota((ROWS, 128), 1)
    own = jnp.where((lax.rem(l128, 16) == r12) & (l128 < 48), rows, 0.0)
    labcol = jnp.sum(jnp.where(l128 < 16, own, 0.0), axis=1, keepdims=True)
    labk[...] = jnp.broadcast_to(jnp.where(labcol > 0.5, labcol, -1.0), (ROWS, 128))
    pick16 = (iota((8, 128), 1) // 16 == iota((8, 128), 0)).astype(F32).astype(BF16)
    rowv[...] = mm(pick16, own.astype(BF16), 1, 1)

    def arrive(kind):
        pltpu.make_async_copy(frecv.at[kind], frecv.at[kind], zrecv.at[kind]).wait()

    def take(kind):
        def unmix(b, carry):
            block = frecv[kind, pl.ds(b * GRP, GRP)].reshape(192, 128)
            got = mm(split, block, 1, 0).astype(BF16)
            at = pl.ds(pl.multiple_of(b * 96, 96), 96)
            xs[kind, at, 0:128] = got[0:96]
            xs[kind, at, 128:256] = got[96:192]
            return carry

        lax.fori_loop(0, NDP // GRP, unmix, 0)

    def give(kind, value):
        def mix(b, carry):
            at = pl.ds(pl.multiple_of(b * 96, 96), 96)
            v = value[at, :].astype(BF16)
            block = jnp.concatenate([v[:, 0:128], v[:, 128:256]], axis=0)
            got = mm(join, block, 1, 0).astype(BF16)
            bsend[kind, pl.ds(b * GRP, GRP)] = got.reshape(GRP, 3, 8, 128)
            return carry

        lax.fori_loop(0, NDP // GRP, mix, 0)

    def back(kind):
        def send(k, carry):
            spread_out(lax.rem(base + k, GRP), bsend.at[kind], brecv.at[kind], bsem_s, bsem_r.at[kind])
            return carry

        lax.fori_loop(1, GRP + 1, send, 0)
        pltpu.make_async_copy(bsend.at[kind, dp], brecv.at[kind, dp], bsem_r.at[kind]).start()

    for kind in range(2):
        arrive(kind)
        take(kind)
    for g in range(2):
        arrive(2 + 2 * g)
        take(2 + 2 * g)
        arrive(3 + 2 * g)
        if g == 1:
            back(0)
        take(3 + 2 * g)

        def attend(b, carry):
            at = pl.ds(pl.multiple_of(b * HD, HD), HD)
            key, val = xs[0], xs[1]
            qb, gb = xs[2 + 2 * g, at, :], xs[3 + 2 * g, at, :]
            s = mm(key, qb, 1, 1) * SCALE
            ok = labk[:, 0:1] == rowv[0:1, at]
            s = jnp.where(ok, s, MASKED)
            top = jnp.max(s, axis=0, keepdims=True)
            e = jnp.exp(s - top)
            p = e * (1.0 / jnp.sum(e, axis=0, keepdims=True))
            d = mm(val, gb, 1, 1) - rowv[1 + g : 2 + g, at]
            ds = (p * d).astype(BF16)
            pv = mm(p.astype(BF16), gb, 1, 0)
            pk = mm(ds, qb, 1, 0)
            if g == 0:
                first = b == 0
                dv_acc[...] = jnp.where(first, 0.0, dv_acc[...]) + pv
                dk_acc[...] = jnp.where(first, 0.0, dk_acc[...]) + pk
            else:
                dv_acc[...] += pv
                dk_acc[...] += pk
            dq_acc[at, :] = mm(ds, key, 0, 0) * SCALE
            return carry

        if g == 0:
            dv_acc[...] = jnp.zeros((ROWS, HD), F32)
            dk_acc[...] = jnp.zeros((ROWS, HD), F32)
        lax.fori_loop(0, ROWS // HD, attend, 0)
        give(g, dq_acc)
    back(1)
    dk_acc[...] = dk_acc[...] * SCALE
    give(2, dk_acc)
    back(2)
    give(3, dv_acc)
    back(3)

    for kind in range(NB):
        pltpu.make_async_copy(brecv.at[kind], brecv.at[kind], bsem_r.at[kind]).wait()
        got = mm(gather[...], brecv[kind].reshape(2 * ROWS, 128), 1, 0).astype(BF16)
        for t in range(NY):
            obuf[kind, t, :, 0:128] = got[t * TOK : (t + 1) * TOK]
            obuf[kind, t, :, 128:256] = got[(NY + t) * TOK : (NY + t + 1) * TOK]
        ref = (oq_ref, oq_ref, ok_ref, ov_ref)[kind]
        if kind < 2:
            cols = pl.ds(pl.multiple_of(y * 2 * HD + kind * HD, HD), HD)
        else:
            cols = pl.ds(pl.multiple_of(y * HD, HD), HD)
        for t in ring_y:
            pltpu.make_async_remote_copy(
                src_ref=obuf.at[kind, t], dst_ref=ref.at[:, cols], send_sem=osem_s, recv_sem=osem_r.at[max(0, kind - 1)],
                device_id=(dp, t), device_id_type=MESH,
            ).start()
        pltpu.make_async_copy(obuf.at[kind, y], ref.at[:, cols], osem_r.at[max(0, kind - 1)]).start()

    pltpu.make_async_copy(oq_ref, oq_ref, osem_r.at[0]).wait()
    pltpu.make_async_copy(ok_ref, ok_ref, osem_r.at[1]).wait()
    pltpu.make_async_copy(ov_ref, ov_ref, osem_r.at[2]).wait()
    some = pl.ds(0, NY - 1)
    pltpu.make_async_copy(meta_r.at[some], meta_r.at[some], ymsend).wait()
    pltpu.make_async_copy(del_r.at[some], del_r.at[some], ydsend).wait()
    pltpu.make_async_copy(tok.at[:, some], tok.at[:, some], ysend).wait()
    pltpu.make_async_copy(obuf.at[:, some], obuf.at[:, some], osem_s).wait()
    most = pl.ds(0, NDP - 1)
    pltpu.make_async_copy(msend.at[most], msend.at[most], zmsend).wait()
    pltpu.make_async_copy(fsend.at[:, most], fsend.at[:, most], zsend).wait()
    pltpu.make_async_copy(bsend.at[:, most], bsend.at[:, most], bsem_s).wait()


def body(queries, key_rows, values, saved_out, out_grad, pack_of, segment_label):
    anywhere = pl.BlockSpec(memory_space=pl.ANY)
    hbm = pl.BlockSpec(memory_space=pltpu.HBM)
    dma = pltpu.SemaphoreType.DMA
    return pl.pallas_call(
        kernel,
        out_shape=(
            jax.ShapeDtypeStruct((TOK, 8 * HD), BF16),
            jax.ShapeDtypeStruct((TOK, 4 * HD), BF16),
            jax.ShapeDtypeStruct((TOK, 4 * HD), BF16),
        ),
        in_specs=[hbm] * 7,
        out_specs=(anywhere,) * 3,
        scratch_shapes=[
            pltpu.VMEM((2, 1, TOK), jnp.int32),
            pltpu.VMEM((TOK, 8 * HD), BF16),
            pltpu.VMEM((TOK, 8 * HD), BF16),
            pltpu.VMEM((NT, NY, TOK, HD), BF16),
            pltpu.VMEM((8, TOK), F32),
            pltpu.VMEM((NY, 8, TOK), F32),
            pltpu.VMEM((NY, 8, TOK), F32),
            pltpu.VMEM((NY, 8, TOK), F32),
            pltpu.VMEM((2 * ROWS, 2 * NY * TOK), BF16),
            pltpu.VMEM((2 * NY * TOK, 2 * ROWS), BF16),
            pltpu.VMEM((NT, NDP, 3, 8, 128), BF16),
            pltpu.VMEM((NT, NDP, 3, 8, 128), BF16),
            pltpu.VMEM((NDP, 1, 128), F32),
            pltpu.VMEM((NDP, 1, 128), F32),
            pltpu.VMEM((NT, ROWS, HD), BF16),
            pltpu.VMEM((8, ROWS), F32),
            pltpu.VMEM((ROWS, 128), F32),
            pltpu.VMEM((ROWS, HD), F32),
            pltpu.VMEM((ROWS, HD), F32),
            pltpu.VMEM((ROWS, HD), F32),
            pltpu.VMEM((NB, NDP, 3, 8, 128), BF16),
            pltpu.VMEM((NB, NDP, 3, 8, 128), BF16),
            pltpu.VMEM((NB, NY, TOK, HD), BF16),
            dma((2,)), dma((2,)), dma, dma((NT,)), dma, dma, dma, dma, dma, dma((NT,)), dma, dma,
            dma, dma((NB,)), dma, dma((3,)),
            pltpu.SemaphoreType.REGULAR, pltpu.SemaphoreType.REGULAR,
        ],
        compiler_params=pltpu.CompilerParams(
            collective_id=0, has_side_effects=True, vmem_limit_bytes=52 << 20
        ),
        name="packed_attention_backward",
    )(
        queries, key_rows, values, out_grad, saved_out,
        pack_of.reshape(1, TOK), segment_label.reshape(1, TOK),
    )


def solution(mesh):
    rows = P(("dp", "ctx"), None)
    return jax.shard_map(
        body,
        mesh=mesh,
        in_specs=(rows, rows, rows, rows, rows, rows, P(("dp", "ctx"))),
        out_specs=(rows, rows, rows),
        check_vma=False,
    )
```

```python
import jax
import jax.numpy as jnp
from jax import lax
from jax.experimental import pallas as pl
from jax.experimental.pallas import tpu as pltpu
from jax.sharding import PartitionSpec as P

MESH = pl.DeviceIdType.MESH
F32 = jnp.float32
BF16 = jnp.bfloat16

NDP = 64
NY = 4
TOK = 128
CAP = 3
HD = 256
SLOT = NY * CAP
ROWS = NDP * SLOT
GRP = 8
PLANE = 16
MASKED = -1e30
SCALE = 1.0 / 16.0

NT, NB = 6, 4


def iota(shape, dim):
    return lax.broadcasted_iota(jnp.int32, shape, dim)


def mm(a, b, ca, cb):
    return lax.dot_general(a, b, (((ca,), (cb,)), ((), ())), preferred_element_type=F32)


def kernel(
    q_ref, k_ref, v_ref, g_ref, o_ref, pack_ref, lab_ref,
    oq_ref, ok_ref, ov_ref,
    ints, gv, ov, tok, meta_s, meta_r, del_s, del_r, place, gather, fsend, frecv, msend, mrecv, xs, rowv, labk,
    dq_acc, dk_acc, dv_acc, bsend, brecv, obuf, fsend2, frecv2, bsend2, brecv2,
    kv, kplace, kgather, ksend, krecv, dksend, dkrecv,
    ksem, kysend, kyrecv, insem, isem, ysend, yrecv, ymsend, ymrecv, ydsend, ydrecv, zsend, zrecv, zmsend, zmrecv,
    bsem_s, bsem_r, osem_s, osem_r, plane_sem, core_sem,
):
    dp = lax.axis_index("dp")
    y = lax.axis_index("ctx")
    x, z, c = dp // 16, lax.rem(dp // 2, 8), lax.rem(dp, 2)
    bar = pltpu.get_barrier_semaphore()

    def at(nx, nz, nc):
        return (nx * 8 + nz) * 2 + nc

    def greet(sem, d, t):
        pl.semaphore_signal(sem, inc=1, device_id=(d, t), device_id_type=MESH)

    ring_x = [at(lax.rem(x + j, 4), z, c) for j in range(1, 4)]
    other = at(x, z, 1 - c)
    ring_y = [lax.rem(y + j, NY) for j in range(1, NY)]
    for t in ring_y:
        greet(bar, dp, t)
    for d in ring_x:
        greet(bar, d, y)
    greet(bar, other, y)
    for j in range(1, 8):
        greet(bar, at(x, lax.rem(z + j, 8), c), y)

    copies = [
        pltpu.make_async_copy(pack_ref, ints.at[0], isem.at[0]),
        pltpu.make_async_copy(lab_ref, ints.at[1], isem.at[1]),
        pltpu.make_async_copy(g_ref, gv, insem.at[0]),
        pltpu.make_async_copy(o_ref, ov, insem.at[1]),
        pltpu.make_async_copy(k_ref, kv, ksem),
    ]
    for n in (0, 1, 4, 2, 3):
        copies[n].start()

    def columns(kind, head):
        if kind == 1:
            return v_ref.at[:, pl.ds(pl.multiple_of(head * HD, HD), HD)]
        ref = q_ref if kind % 2 == 0 else g_ref
        return ref.at[:, pl.ds(pl.multiple_of(head * 2 * HD + (kind // 2 - 1) * HD, HD), HD)]

    for kind in range(1, NT):
        pltpu.make_async_copy(columns(kind, y), tok.at[kind, y], yrecv.at[kind]).start()

    eye = (iota((TOK, TOK), 0) == iota((TOK, TOK), 1)).astype(F32).astype(BF16)
    copies[0].wait()
    copies[1].wait()
    prow = ints[0].astype(F32)
    pcol = mm(eye, jnp.broadcast_to(prow, (8, TOK)).astype(BF16), 1, 1)[:, 0:1]
    earlier = (pcol == prow) & (iota((TOK, TOK), 0) < iota((TOK, TOK), 1))
    rank = jnp.sum(earlier.astype(F32), axis=0, keepdims=True)
    slot = rank + (y * CAP).astype(F32)
    meta_s[0:1, :] = prow
    meta_s[1:2, :] = slot
    meta_s[2:3, :] = ints[1].astype(F32) + 1.0
    meta_s[3:8, :] = jnp.zeros((5, TOK), F32)
    meta_r[y] = meta_s[...]

    pl.semaphore_wait(bar, 14)

    for t in ring_y:
        pltpu.make_async_remote_copy(
            src_ref=meta_s, dst_ref=meta_r.at[y], send_sem=ymsend, recv_sem=ymrecv,
            device_id=(dp, t), device_id_type=MESH,
        ).start()
    for kind in range(1, NT):
        for t in ring_y:
            pltpu.make_async_remote_copy(
                src_ref=columns(kind, t), dst_ref=tok.at[kind, y], send_sem=ysend, recv_sem=yrecv.at[kind],
                device_id=(dp, t), device_id_type=MESH,
            ).start()

    for d in ring_x:
        greet(plane_sem, d, y)
    pl.semaphore_wait(plane_sem, 3)
    greet(core_sem, other, y)
    pl.semaphore_wait(core_sem, 1)

    own_row = (prow * (2.0 * SLOT) + rank).astype(jnp.int32)

    def kplace_block(b, carry):
        r = iota((HD, TOK), 0) + b * HD
        at = pl.ds(pl.multiple_of(b * HD, HD), HD)
        for cb in range(8):
            kplace[at, cb * TOK : (cb + 1) * TOK] = (r == own_row + CAP * cb).astype(F32).astype(BF16)
        return carry

    lax.fori_loop(0, 2 * ROWS // HD, kplace_block, 0)

    spin = [lax.rem(dp + j, PLANE) for j in range(PLANE)]

    def plane(k):
        return lax.rem(x + k, 4)

    def spread_out(g, first, src, dst, ssem, rsem):
        for j in range(first, PLANE):
            d = g * PLANE + spin[j]
            pltpu.make_async_remote_copy(
                src_ref=src.at[d], dst_ref=dst.at[dp], send_sem=ssem, recv_sem=rsem,
                device_id=(d, y), device_id_type=MESH,
            ).start()

    copies[4].wait()

    def fill_k(g):
        at = pl.ds(pl.multiple_of(g * 24 * PLANE, 24 * PLANE), 24 * PLANE)
        stack = jnp.concatenate([kv[:, cb * TOK : (cb + 1) * TOK] for cb in range(8)], axis=0)
        got = mm(kplace[at, :], stack, 1, 0)
        fsend[0, pl.ds(g * PLANE, PLANE)] = got.astype(BF16).reshape(PLANE, 3, 8, 128)

    def step_k(k, carry):
        fill_k(plane(k))
        spread_out(plane(k), 0, fsend.at[0], frecv.at[0], zsend, zrecv.at[0])
        return carry

    lax.fori_loop(1, 4, step_k, 0)
    fill_k(x)
    spread_out(x, 1, fsend.at[0], frecv.at[0], zsend, zrecv.at[0])
    pltpu.make_async_copy(fsend.at[0, dp], frecv.at[0, dp], zrecv.at[0]).start()

    pltpu.make_async_copy(meta_r.at[pl.ds(0, NY - 1)], meta_r.at[pl.ds(0, NY - 1)], ymrecv).wait()
    packs = jnp.concatenate([meta_r[t, 0:1, :] for t in range(NY)], axis=1)
    slots = jnp.concatenate([meta_r[t, 1:2, :] for t in range(NY)], axis=1)
    where = (packs * (2.0 * SLOT) + slots).astype(jnp.int32)

    def place_block(b, carry):
        r = iota((HD, NY * TOK), 0) + b * HD
        at = pl.ds(pl.multiple_of(b * HD, HD), HD)
        place[at, 0 : NY * TOK] = (r == where).astype(F32).astype(BF16)
        place[at, NY * TOK : 2 * NY * TOK] = (r == where + SLOT).astype(F32).astype(BF16)
        return carry

    lax.fori_loop(0, 2 * ROWS // HD, place_block, 0)

    def everyone(src, dst, ssem, rsem):
        def send(k, carry):
            spread_out(plane(k), 0, src, dst, ssem, rsem)
            return carry

        lax.fori_loop(1, 4, send, 0)
        spread_out(x, 1, src, dst, ssem, rsem)
        pltpu.make_async_copy(src.at[dp], dst.at[dp], rsem).start()

    def landed(kind):
        pltpu.make_async_copy(tok.at[kind], tok.at[kind], yrecv.at[kind]).wait()

    def weave(kind):
        t = tok[kind].reshape(NY * TOK, HD)
        return jnp.concatenate([t[:, 0:128], t[:, 128:256]], axis=0)

    def placed(g):
        return place[pl.ds(pl.multiple_of(g * 24 * PLANE, 24 * PLANE), 24 * PLANE), :]

    def forward(kind):
        landed(kind)

        def fill(g):
            got = mm(placed(g), weave(kind), 1, 0)
            fsend[kind, pl.ds(g * PLANE, PLANE)] = got.astype(BF16).reshape(PLANE, 3, 8, 128)

        def step(k, carry):
            fill(plane(k))
            spread_out(plane(k), 0, fsend.at[kind], frecv.at[kind], zsend, zrecv.at[kind])
            return carry

        lax.fori_loop(1, 4, step, 0)
        fill(x)
        spread_out(x, 1, fsend.at[kind], frecv.at[kind], zsend, zrecv.at[kind])
        pltpu.make_async_copy(fsend.at[kind, dp], frecv.at[kind, dp], zrecv.at[kind]).start()

    def forward2(h):
        landed(2 + 2 * h)
        landed(3 + 2 * h)

        def fill(g):
            both = jnp.concatenate([weave(2 + 2 * h), weave(3 + 2 * h)], axis=1)
            got = mm(placed(g), both, 1, 0).astype(BF16)
            here = pl.ds(g * PLANE, PLANE)
            fsend2[h, here, 0:3] = got[:, 0:128].reshape(PLANE, 3, 8, 128)
            fsend2[h, here, 3:6] = got[:, 128:256].reshape(PLANE, 3, 8, 128)

        def step(k, carry):
            fill(plane(k))
            spread_out(plane(k), 0, fsend2.at[h], frecv2.at[h], zsend, zrecv.at[2 + h])
            return carry

        lax.fori_loop(1, 4, step, 0)
        fill(x)
        spread_out(x, 1, fsend2.at[h], frecv2.at[h], zsend, zrecv.at[2 + h])
        pltpu.make_async_copy(fsend2.at[h, dp], frecv2.at[h, dp], zrecv.at[2 + h]).start()

    for kind in range(4):
        if kind == 1:
            forward(kind)
        elif kind > 1:
            forward2(kind - 2)
        if kind == 0:
            copies[2].wait()
            copies[3].wait()
            prod = gv[...].astype(F32) * ov[...].astype(F32)
            hi = prod.astype(BF16)
            lo = (prod - hi.astype(F32)).astype(BF16)
            pick = (iota((8, 8 * HD), 1) // HD == iota((8, 8 * HD), 0)).astype(BF16)
            delta = (mm(pick, hi, 1, 1) + mm(pick, lo, 1, 1)).astype(BF16).astype(F32)
            for t in range(NY):
                del_s[t, 0:2, :] = delta[2 * t : 2 * t + 2, :]
                del_s[t, 2:8, :] = jnp.zeros((6, TOK), F32)
            del_r[y] = del_s[y]
            for t in ring_y:
                pltpu.make_async_remote_copy(
                    src_ref=del_s.at[t], dst_ref=del_r.at[y], send_sem=ydsend, recv_sem=ydrecv,
                    device_id=(dp, t), device_id_type=MESH,
                ).start()
        if kind == 1:
            pltpu.make_async_copy(del_r.at[pl.ds(0, NY - 1)], del_r.at[pl.ds(0, NY - 1)], ydrecv).wait()
            owner = (iota((NDP, NY * TOK), 0).astype(F32) == packs).astype(F32).astype(BF16)
            lane = iota((128, NY * TOK), 0)
            vals = [jnp.concatenate([meta_r[t, 2:3, :] for t in range(NY)], axis=1)]
            vals += [jnp.concatenate([del_r[t, j : j + 1, :] for t in range(NY)], axis=1) for j in range(2)]
            kindv = jnp.where(lane // 16 == 0, vals[0], jnp.where(lane // 16 == 1, vals[1], vals[2]))
            hit = (lax.rem(lane, 16).astype(F32) == slots) & (lane < 48)
            small = jnp.where(hit, kindv, 0.0).astype(BF16)
            msend[...] = mm(owner, small, 1, 1).reshape(NDP, 1, 128)

            everyone(msend, mrecv, zmsend, zmrecv)

    for t in range(NY):
        col = mm(eye, meta_r[t].astype(BF16), 1, 1)
        home = (col[:, 0:1] * (2.0 * SLOT) + col[:, 1:2]).astype(jnp.int32)
        for half in range(2):
            row = half * NY * TOK + t * TOK

            def gather_block(b, carry):
                r = iota((TOK, HD), 1) + b * HD
                gather[row : row + TOK, pl.ds(pl.multiple_of(b * HD, HD), HD)] = (
                    (r == home + half * SLOT).astype(F32).astype(BF16)
                )
                return carry

            lax.fori_loop(0, 2 * ROWS // HD, gather_block, 0)

    own_col = mm(eye, jnp.broadcast_to(prow, (8, TOK)).astype(BF16), 1, 1)[:, 0:1] * (2.0 * SLOT)
    own_col = (own_col + mm(eye, jnp.broadcast_to(rank, (8, TOK)).astype(BF16), 1, 1)[:, 0:1]).astype(jnp.int32)

    def kgather_block(b, carry):
        r = iota((TOK, HD), 1) + b * HD
        at = pl.ds(pl.multiple_of(b * HD, HD), HD)
        for cb in range(8):
            kgather[cb * TOK : (cb + 1) * TOK, at] = (r == own_col + CAP * cb).astype(F32).astype(BF16)
        return carry

    lax.fori_loop(0, 2 * ROWS // HD, kgather_block, 0)

    def by_head(r):
        return (lax.rem(r, 24) // 3) * 24 + (r // 48) * 6 + (lax.rem(r, 48) // 24) * 3 + lax.rem(r, 3)

    def by_ctx(r):
        return (lax.rem(r, 12) // 3) * 48 + (r // 96) * 24 + (lax.rem(r, 96) // 12) * 3 + lax.rem(r, 3)

    ia, ib = iota((192, 192), 0), iota((192, 192), 1)
    head_out = (ib == by_head(ia)).astype(F32).astype(BF16)
    head_in = (ia == by_head(ib)).astype(F32).astype(BF16)
    ctx_out = (ib == by_ctx(ia)).astype(F32).astype(BF16)
    ctx_in = (ia == by_ctx(ib)).astype(F32).astype(BF16)

    def exchange(src, dst, rsem):
        for t in ring_y:
            pltpu.make_async_remote_copy(
                src_ref=src.at[t], dst_ref=dst.at[y], send_sem=kysend, recv_sem=rsem,
                device_id=(dp, t), device_id_type=MESH,
            ).start()
        pltpu.make_async_copy(src.at[y], dst.at[y], rsem).start()

    pltpu.make_async_copy(frecv.at[0], frecv.at[0], zrecv.at[0]).wait()

    def deal(b, carry):
        got = mm(head_out, frecv[0, pl.ds(b * GRP, GRP)].reshape(192, 128), 1, 0).astype(BF16)
        at = pl.ds(pl.multiple_of(b * 48, 48), 48)
        for t in range(NY):
            ksend[t, at, :] = got[48 * t : 48 * t + 48]
        return carry

    lax.fori_loop(0, NDP // GRP, deal, 0)
    exchange(ksend, krecv, kyrecv.at[0])

    a, b = iota((192, 192), 0), iota((192, 192), 1)
    split = (b == (lax.rem(a, 96) // 12) * 24 + (a // 96) * 12 + lax.rem(a, 12)).astype(F32).astype(BF16)
    join = (a == (lax.rem(b, 96) // 12) * 24 + (b // 96) * 12 + lax.rem(b, 12)).astype(F32).astype(BF16)

    pltpu.make_async_copy(mrecv, mrecv, zmrecv).wait()
    spread = (iota((ROWS, NDP), 0) // SLOT == iota((ROWS, NDP), 1)).astype(F32).astype(BF16)
    rows = mm(spread, mrecv[...].reshape(NDP, 128).astype(BF16), 1, 0)
    r12, l128 = lax.rem(iota((ROWS, 128), 0), SLOT), iota((ROWS, 128), 1)
    own = jnp.where((lax.rem(l128, 16) == r12) & (l128 < 48), rows, 0.0)
    labcol = jnp.sum(jnp.where(l128 < 16, own, 0.0), axis=1, keepdims=True)
    labk[...] = jnp.broadcast_to(jnp.where(labcol > 0.5, labcol, -1.0), (ROWS, 128))
    pick16 = (iota((8, 128), 1) // 16 == iota((8, 128), 0)).astype(F32).astype(BF16)
    rowv[...] = mm(pick16, own.astype(BF16), 1, 1)

    def take(kind):
        pltpu.make_async_copy(frecv.at[kind], frecv.at[kind], zrecv.at[kind]).wait()

        def unmix(b, carry):
            block = frecv[kind, pl.ds(b * GRP, GRP)].reshape(192, 128)
            got = mm(split, block, 1, 0).astype(BF16)
            at = pl.ds(pl.multiple_of(b * 96, 96), 96)
            xs[kind, at, 0:128] = got[0:96]
            xs[kind, at, 128:256] = got[96:192]
            return carry

        lax.fori_loop(0, NDP // GRP, unmix, 0)

    def take2(h):
        def unmix(b, carry):
            here = pl.ds(b * GRP, GRP)
            block = jnp.concatenate(
                [frecv2[h, here, 0:3].reshape(192, 128), frecv2[h, here, 3:6].reshape(192, 128)], axis=1
            )
            got = mm(split, block, 1, 0).astype(BF16)
            at = pl.ds(pl.multiple_of(b * 96, 96), 96)
            for j in range(2):
                xs[2 + 2 * h + j, at, 0:128] = got[0:96, 128 * j : 128 * j + 128]
                xs[2 + 2 * h + j, at, 128:256] = got[96:192, 128 * j : 128 * j + 128]
            return carry

        lax.fori_loop(0, NDP // GRP, unmix, 0)

    def halves_of(value, at):
        v = value[at, :].astype(BF16)
        return jnp.concatenate([v[:, 0:128], v[:, 128:256]], axis=0)

    def give(kind):
        def mix(b, carry):
            at = pl.ds(pl.multiple_of(b * 96, 96), 96)
            got = mm(join, halves_of(dq_acc, at), 1, 0).astype(BF16)
            bsend[kind, pl.ds(b * GRP, GRP)] = got.reshape(GRP, 3, 8, 128)
            return carry

        lax.fori_loop(0, NDP // GRP, mix, 0)

    def give2():
        def mix(b, carry):
            at = pl.ds(pl.multiple_of(b * 96, 96), 96)
            both = jnp.concatenate([halves_of(dq_acc, at), halves_of(dv_acc, at)], axis=1)
            got = mm(join, both, 1, 0).astype(BF16)
            here = pl.ds(b * GRP, GRP)
            bsend2[here, 0:3] = got[:, 0:128].reshape(GRP, 3, 8, 128)
            bsend2[here, 3:6] = got[:, 128:256].reshape(GRP, 3, 8, 128)
            return carry

        lax.fori_loop(0, NDP // GRP, mix, 0)

    take(1)
    pltpu.make_async_copy(krecv, krecv, kyrecv.at[0]).wait()

    def collect(b, carry):
        at = pl.ds(pl.multiple_of(b * 48, 48), 48)
        got = mm(ctx_out, jnp.concatenate([krecv[t, at, :] for t in range(NY)], axis=0), 1, 0).astype(BF16)
        at = pl.ds(pl.multiple_of(b * 96, 96), 96)
        xs[0, at, 0:128] = got[0:96]
        xs[0, at, 128:256] = got[96:192]
        return carry

    lax.fori_loop(0, NDP // GRP, collect, 0)
    for g in range(2):
        pltpu.make_async_copy(frecv2.at[g], frecv2.at[g], zrecv.at[2 + g]).wait()
        if g == 1:
            everyone(bsend.at[0], brecv.at[0], bsem_s, bsem_r.at[0])
        take2(g)

        def attend(b, carry):
            at = pl.ds(pl.multiple_of(b * HD, HD), HD)
            key, val = xs[0], xs[1]
            qb, gb = xs[2 + 2 * g, at, :], xs[3 + 2 * g, at, :]
            s = mm(key, qb, 1, 1) * SCALE
            ok = labk[:, 0:1] == rowv[0:1, at]
            s = jnp.where(ok, s, MASKED)
            top = jnp.max(s, axis=0, keepdims=True)
            e = jnp.exp(s - top)
            p = e * (1.0 / jnp.sum(e, axis=0, keepdims=True))
            d = mm(val, gb, 1, 1) - rowv[1 + g : 2 + g, at]
            ds = (p * d).astype(BF16)
            pv = mm(p.astype(BF16), gb, 1, 0)
            pk = mm(ds, qb, 1, 0)
            if g == 0:
                first = b == 0
                dv_acc[...] = jnp.where(first, 0.0, dv_acc[...]) + pv
                dk_acc[...] = jnp.where(first, 0.0, dk_acc[...]) + pk
            else:
                dv_acc[...] += pv
                dk_acc[...] += pk
            dq_acc[at, :] = mm(ds, key, 0, 0) * SCALE
            return carry

        if g == 0:
            dv_acc[...] = jnp.zeros((ROWS, HD), F32)
            dk_acc[...] = jnp.zeros((ROWS, HD), F32)
        lax.fori_loop(0, ROWS // HD, attend, 0)
        if g == 0:
            give(0)
    def deal_back(b, carry):
        at = pl.ds(pl.multiple_of(b * 96, 96), 96)
        v = (dk_acc[at, :] * SCALE).astype(BF16)
        got = mm(ctx_in, jnp.concatenate([v[:, 0:128], v[:, 128:256]], axis=0), 1, 0).astype(BF16)
        at = pl.ds(pl.multiple_of(b * 48, 48), 48)
        for t in range(NY):
            dksend[t, at, :] = got[48 * t : 48 * t + 48]
        return carry

    lax.fori_loop(0, NDP // GRP, deal_back, 0)
    exchange(dksend, dkrecv, kyrecv.at[1])
    give2()
    everyone(bsend2, brecv2, bsem_s, bsem_r.at[1])
    pltpu.make_async_copy(dkrecv, dkrecv, kyrecv.at[1]).wait()

    def collect_back(b, carry):
        at = pl.ds(pl.multiple_of(b * 48, 48), 48)
        got = mm(head_in, jnp.concatenate([dkrecv[t, at, :] for t in range(NY)], axis=0), 1, 0).astype(BF16)
        bsend[1, pl.ds(b * GRP, GRP)] = got.reshape(GRP, 3, 8, 128)
        return carry

    lax.fori_loop(0, NDP // GRP, collect_back, 0)
    everyone(bsend.at[1], brecv.at[1], bsem_s, bsem_r.at[2])

    def home(kind, got, ref, col, sem):
        for t in range(NY):
            obuf[kind, t, :, 0:128] = got[t * TOK : (t + 1) * TOK]
            obuf[kind, t, :, 128:256] = got[(NY + t) * TOK : (NY + t + 1) * TOK]
        cols = pl.ds(pl.multiple_of(col, HD), HD)
        for t in ring_y:
            pltpu.make_async_remote_copy(
                src_ref=obuf.at[kind, t], dst_ref=ref.at[:, cols], send_sem=osem_s, recv_sem=sem,
                device_id=(dp, t), device_id_type=MESH,
            ).start()
        pltpu.make_async_copy(obuf.at[kind, y], ref.at[:, cols], sem).start()

    pltpu.make_async_copy(brecv.at[0], brecv.at[0], bsem_r.at[0]).wait()
    got = mm(gather[...], brecv[0].reshape(2 * ROWS, 128), 1, 0).astype(BF16)
    home(0, got, oq_ref, y * 2 * HD, osem_r.at[0])
    pltpu.make_async_copy(brecv2, brecv2, bsem_r.at[1]).wait()
    both = jnp.concatenate(
        [brecv2[:, 0:3].reshape(2 * ROWS, 128), brecv2[:, 3:6].reshape(2 * ROWS, 128)], axis=1
    )
    got = mm(gather[...], both, 1, 0).astype(BF16)
    home(1, got[:, 0:128], oq_ref, y * 2 * HD + HD, osem_r.at[0])
    home(2, got[:, 128:256], ov_ref, y * HD, osem_r.at[2])
    pltpu.make_async_copy(brecv.at[1], brecv.at[1], bsem_r.at[2]).wait()
    got = mm(kgather[...], brecv[1].reshape(2 * ROWS, 128), 1, 0).astype(BF16)
    for cb in range(8):
        kv[:, cb * TOK : (cb + 1) * TOK] = got[cb * TOK : (cb + 1) * TOK]
    pltpu.make_async_copy(kv, ok_ref, osem_r.at[1]).start()

    pltpu.make_async_copy(oq_ref, oq_ref, osem_r.at[0]).wait()
    pltpu.make_async_copy(ok_ref, ok_ref, osem_r.at[1]).wait()
    pltpu.make_async_copy(ov_ref, ov_ref, osem_r.at[2]).wait()
    some = pl.ds(0, NY - 1)
    pltpu.make_async_copy(meta_r.at[some], meta_r.at[some], ymsend).wait()
    pltpu.make_async_copy(del_r.at[some], del_r.at[some], ydsend).wait()
    pltpu.make_async_copy(tok.at[1:NT, some], tok.at[1:NT, some], ysend).wait()
    pltpu.make_async_copy(ksend.at[some], ksend.at[some], kysend).wait()
    pltpu.make_async_copy(dksend.at[some], dksend.at[some], kysend).wait()
    pltpu.make_async_copy(obuf.at[0:3, some], obuf.at[0:3, some], osem_s).wait()
    most = pl.ds(0, NDP - 1)
    pltpu.make_async_copy(msend.at[most], msend.at[most], zmsend).wait()
    pltpu.make_async_copy(fsend.at[:, most], fsend.at[:, most], zsend).wait()
    pltpu.make_async_copy(fsend2.at[:, most], fsend2.at[:, most], zsend).wait()
    pltpu.make_async_copy(bsend.at[:, most], bsend.at[:, most], bsem_s).wait()
    pltpu.make_async_copy(bsend2.at[most], bsend2.at[most], bsem_s).wait()


def body(queries, key_rows, values, saved_out, out_grad, pack_of, segment_label):
    anywhere = pl.BlockSpec(memory_space=pl.ANY)
    hbm = pl.BlockSpec(memory_space=pltpu.HBM)
    dma = pltpu.SemaphoreType.DMA
    return pl.pallas_call(
        kernel,
        out_shape=(
            jax.ShapeDtypeStruct((TOK, 8 * HD), BF16),
            jax.ShapeDtypeStruct((TOK, 4 * HD), BF16),
            jax.ShapeDtypeStruct((TOK, 4 * HD), BF16),
        ),
        in_specs=[hbm] * 7,
        out_specs=(anywhere,) * 3,
        scratch_shapes=[
            pltpu.VMEM((2, 1, TOK), jnp.int32),
            pltpu.VMEM((TOK, 8 * HD), BF16),
            pltpu.VMEM((TOK, 8 * HD), BF16),
            pltpu.VMEM((NT, NY, TOK, HD), BF16),
            pltpu.VMEM((8, TOK), F32),
            pltpu.VMEM((NY, 8, TOK), F32),
            pltpu.VMEM((NY, 8, TOK), F32),
            pltpu.VMEM((NY, 8, TOK), F32),
            pltpu.VMEM((2 * ROWS, 2 * NY * TOK), BF16),
            pltpu.VMEM((2 * NY * TOK, 2 * ROWS), BF16),
            pltpu.VMEM((2, NDP, 3, 8, 128), BF16),
            pltpu.VMEM((2, NDP, 3, 8, 128), BF16),
            pltpu.VMEM((NDP, 1, 128), F32),
            pltpu.VMEM((NDP, 1, 128), F32),
            pltpu.VMEM((NT, ROWS, HD), BF16),
            pltpu.VMEM((8, ROWS), F32),
            pltpu.VMEM((ROWS, 128), F32),
            pltpu.VMEM((ROWS, HD), F32),
            pltpu.VMEM((ROWS, HD), F32),
            pltpu.VMEM((ROWS, HD), F32),
            pltpu.VMEM((2, NDP, 3, 8, 128), BF16),
            pltpu.VMEM((2, NDP, 3, 8, 128), BF16),
            pltpu.VMEM((NB, NY, TOK, HD), BF16),
            pltpu.VMEM((2, NDP, 6, 8, 128), BF16),
            pltpu.VMEM((2, NDP, 6, 8, 128), BF16),
            pltpu.VMEM((NDP, 6, 8, 128), BF16),
            pltpu.VMEM((NDP, 6, 8, 128), BF16),
            pltpu.VMEM((TOK, 4 * HD), BF16),
            pltpu.VMEM((2 * ROWS, 8 * TOK), BF16),
            pltpu.VMEM((8 * TOK, 2 * ROWS), BF16),
            pltpu.VMEM((NY, 2 * 192, 128), BF16),
            pltpu.VMEM((NY, 2 * 192, 128), BF16),
            pltpu.VMEM((NY, 2 * 192, 128), BF16),
            pltpu.VMEM((NY, 2 * 192, 128), BF16),
            dma, dma, dma((2,)), dma((2,)), dma((2,)), dma, dma((NT,)), dma, dma, dma, dma, dma, dma((4,)), dma, dma,
            dma, dma((3,)), dma, dma((3,)),
            pltpu.SemaphoreType.REGULAR, pltpu.SemaphoreType.REGULAR,
        ],
        compiler_params=pltpu.CompilerParams(
            collective_id=0, has_side_effects=True, vmem_limit_bytes=63 << 20
        ),
        name="packed_attention_backward",
    )(
        queries, key_rows, values, out_grad, saved_out,
        pack_of.reshape(1, TOK), segment_label.reshape(1, TOK),
    )


def solution(mesh):
    rows = P(("dp", "ctx"), None)
    return jax.shard_map(
        body,
        mesh=mesh,
        in_specs=(rows, rows, rows, rows, rows, rows, P(("dp", "ctx"))),
        out_specs=(rows, rows, rows),
        check_vma=False,
    )
```

```python
import jax
import jax.numpy as jnp
from jax import lax
from jax.experimental import pallas as pl
from jax.experimental.pallas import tpu as pltpu
from jax.sharding import PartitionSpec as P

MESH = pl.DeviceIdType.MESH
F32 = jnp.float32
BF16 = jnp.bfloat16

NDP = 64
NY = 4
TOK = 128
CAP = 3
HD = 256
SLOT = NY * CAP
ROWS = NDP * SLOT
GRP = 8
PLANE = 16
EARLY = 3
MASKED = -1e30
SCALE = 1.0 / 16.0

NT = 6


def iota(shape, dim):
    return lax.broadcasted_iota(jnp.int32, shape, dim)


def mm(a, b, ca, cb):
    return lax.dot_general(a, b, (((ca,), (cb,)), ((), ())), preferred_element_type=F32)


def kernel(
    q_ref, k_ref, v_ref, g_ref, o_ref, pack_ref, lab_ref,
    oq_ref, ok_ref, ov_ref,
    ints, gv, ov, tok, meta_s, meta_r, del_s, del_r, place, gather, fsend, frecv, msend, mrecv, xs, rowv, labk,
    dq_acc, dk_acc, dv_acc, bsend, brecv, obuf, fsend2, frecv2, kvout,
    kv, kplace, kgather, ksend, krecv, dksend, dkrecv,
    ksem, kysend, kyrecv, insem, isem, ysend, yrecv, ymsend, ymrecv, ydsend, ydrecv, zsend, zrecv, zmsend, zmrecv,
    bsem_s, bsem_r, osem_s, osem_r, plane_sem, core_sem,
):
    dp = lax.axis_index("dp")
    y = lax.axis_index("ctx")
    x, z, c = dp // 16, lax.rem(dp // 2, 8), lax.rem(dp, 2)
    bar = pltpu.get_barrier_semaphore()

    def at(nx, nz, nc):
        return (nx * 8 + nz) * 2 + nc

    def greet(sem, d, t):
        pl.semaphore_signal(sem, inc=1, device_id=(d, t), device_id_type=MESH)

    ring_x = [at(lax.rem(x + j, 4), z, c) for j in range(1, 4)]
    other = at(x, z, 1 - c)
    ring_y = [lax.rem(y + j, NY) for j in range(1, NY)]
    for t in ring_y:
        greet(bar, dp, t)
    for d in ring_x:
        greet(bar, d, y)
    greet(bar, other, y)
    for j in range(1, 8):
        greet(bar, at(x, lax.rem(z + j, 8), c), y)

    copies = [
        pltpu.make_async_copy(pack_ref, ints.at[0], isem.at[0]),
        pltpu.make_async_copy(lab_ref, ints.at[1], isem.at[1]),
        pltpu.make_async_copy(g_ref, gv, insem.at[0]),
        pltpu.make_async_copy(o_ref, ov, insem.at[1]),
        pltpu.make_async_copy(k_ref, kv, ksem),
    ]
    for n in (0, 1, 4, 2, 3):
        copies[n].start()

    def columns(kind, head):
        if kind == 1:
            return v_ref.at[:, pl.ds(pl.multiple_of(head * HD, HD), HD)]
        ref = q_ref if kind % 2 == 0 else g_ref
        return ref.at[:, pl.ds(pl.multiple_of(head * 2 * HD + (kind // 2 - 1) * HD, HD), HD)]

    for kind in range(1, NT):
        pltpu.make_async_copy(columns(kind, y), tok.at[kind, y], yrecv.at[kind]).start()

    eye = (iota((TOK, TOK), 0) == iota((TOK, TOK), 1)).astype(F32).astype(BF16)
    copies[0].wait()
    copies[1].wait()
    prow = ints[0].astype(F32)
    pcol = mm(eye, jnp.broadcast_to(prow, (8, TOK)).astype(BF16), 1, 1)[:, 0:1]
    earlier = (pcol == prow) & (iota((TOK, TOK), 0) < iota((TOK, TOK), 1))
    rank = jnp.sum(earlier.astype(F32), axis=0, keepdims=True)
    slot = rank + (y * CAP).astype(F32)
    meta_s[0:1, :] = prow
    meta_s[1:2, :] = slot
    meta_s[2:3, :] = ints[1].astype(F32) + 1.0
    meta_s[3:8, :] = jnp.zeros((5, TOK), F32)
    meta_r[y] = meta_s[...]

    pl.semaphore_wait(bar, 14)

    for d in ring_x:
        greet(plane_sem, d, y)

    for t in ring_y:
        pltpu.make_async_remote_copy(
            src_ref=meta_s, dst_ref=meta_r.at[y], send_sem=ymsend, recv_sem=ymrecv,
            device_id=(dp, t), device_id_type=MESH,
        ).start()
    for kind in range(1, NT):
        for t in ring_y:
            pltpu.make_async_remote_copy(
                src_ref=columns(kind, t), dst_ref=tok.at[kind, y], send_sem=ysend, recv_sem=yrecv.at[kind],
                device_id=(dp, t), device_id_type=MESH,
            ).start()

    own_row = (prow * (2.0 * SLOT) + rank).astype(jnp.int32)

    def kplace_block(b, carry):
        r = iota((HD, TOK), 0) + b * HD
        at = pl.ds(pl.multiple_of(b * HD, HD), HD)
        for cb in range(8):
            kplace[at, cb * TOK : (cb + 1) * TOK] = (r == own_row + CAP * cb).astype(F32).astype(BF16)
        return carry

    lax.fori_loop(0, 2 * ROWS // HD, kplace_block, 0)

    pl.semaphore_wait(plane_sem, 3)
    greet(core_sem, other, y)

    spin = [lax.rem(dp + j, PLANE) for j in range(PLANE)]

    def plane(k):
        return lax.rem(x + k, 4)

    def spread_out(g, first, src, dst, ssem, rsem):
        for j in range(first, PLANE):
            d = g * PLANE + spin[j]
            pltpu.make_async_remote_copy(
                src_ref=src.at[d], dst_ref=dst.at[dp], send_sem=ssem, recv_sem=rsem,
                device_id=(d, y), device_id_type=MESH,
            ).start()

    copies[4].wait()

    def fill_k(g):
        at = pl.ds(pl.multiple_of(g * 24 * PLANE, 24 * PLANE), 24 * PLANE)
        stack = jnp.concatenate([kv[:, cb * TOK : (cb + 1) * TOK] for cb in range(8)], axis=0)
        got = mm(kplace[at, :], stack, 1, 0)
        fsend[0, pl.ds(g * PLANE, PLANE)] = got.astype(BF16).reshape(PLANE, 3, 8, 128)

    def step_k(k, carry):
        spread_out(plane(k), 0, fsend.at[0], frecv.at[0], zsend, zrecv.at[0])
        fill_k(plane(k + 1))
        return carry

    fill_k(plane(1))
    pl.semaphore_wait(core_sem, 1)
    lax.fori_loop(1, 4, step_k, 0)
    spread_out(x, 1, fsend.at[0], frecv.at[0], zsend, zrecv.at[0])
    pltpu.make_async_copy(fsend.at[0, dp], frecv.at[0, dp], zrecv.at[0]).start()

    pltpu.make_async_copy(meta_r.at[pl.ds(0, NY - 1)], meta_r.at[pl.ds(0, NY - 1)], ymrecv).wait()
    packs = jnp.concatenate([meta_r[t, 0:1, :] for t in range(NY)], axis=1)
    slots = jnp.concatenate([meta_r[t, 1:2, :] for t in range(NY)], axis=1)
    where = (packs * (2.0 * SLOT) + slots).astype(jnp.int32)

    def place_block(b, carry):
        r = iota((HD, NY * TOK), 0) + b * HD
        at = pl.ds(pl.multiple_of(b * HD, HD), HD)
        place[at, 0 : NY * TOK] = (r == where).astype(F32).astype(BF16)
        place[at, NY * TOK : 2 * NY * TOK] = (r == where + SLOT).astype(F32).astype(BF16)
        return carry

    lax.fori_loop(0, 2 * ROWS // HD, place_block, 0)

    def everyone(src, dst, ssem, rsem, done=0):
        def send(k, carry):
            spread_out(plane(k), 0, src, dst, ssem, rsem)
            return carry

        lax.fori_loop(1 + done, 4, send, 0)
        spread_out(x, 1, src, dst, ssem, rsem)
        pltpu.make_async_copy(src.at[dp], dst.at[dp], rsem).start()

    def landed(kind):
        pltpu.make_async_copy(tok.at[kind], tok.at[kind], yrecv.at[kind]).wait()

    def weave(kind):
        t = tok[kind].reshape(NY * TOK, HD)
        return jnp.concatenate([t[:, 0:128], t[:, 128:256]], axis=0)

    def placed(g):
        return place[pl.ds(pl.multiple_of(g * 24 * PLANE, 24 * PLANE), 24 * PLANE), :]

    def forward(kind):
        landed(kind)

        def fill(g):
            got = mm(placed(g), weave(kind), 1, 0)
            fsend[kind, pl.ds(g * PLANE, PLANE)] = got.astype(BF16).reshape(PLANE, 3, 8, 128)

        def step(k, carry):
            fill(plane(k))
            spread_out(plane(k), 0, fsend.at[kind], frecv.at[kind], zsend, zrecv.at[kind])
            return carry

        lax.fori_loop(1, 4, step, 0)
        fill(x)
        spread_out(x, 1, fsend.at[kind], frecv.at[kind], zsend, zrecv.at[kind])
        pltpu.make_async_copy(fsend.at[kind, dp], frecv.at[kind, dp], zrecv.at[kind]).start()

    def forward2(h):
        landed(2 + 2 * h)
        landed(3 + 2 * h)

        def fill(g):
            both = jnp.concatenate([weave(2 + 2 * h), weave(3 + 2 * h)], axis=1)
            got = mm(placed(g), both, 1, 0).astype(BF16)
            here = pl.ds(g * PLANE, PLANE)
            fsend2[h, here, 0:3] = got[:, 0:128].reshape(PLANE, 3, 8, 128)
            fsend2[h, here, 3:6] = got[:, 128:256].reshape(PLANE, 3, 8, 128)

        def step(k, carry):
            fill(plane(k))
            spread_out(plane(k), 0, fsend2.at[h], frecv2.at[h], zsend, zrecv.at[2 + h])
            return carry

        lax.fori_loop(1, 4, step, 0)
        fill(x)
        spread_out(x, 1, fsend2.at[h], frecv2.at[h], zsend, zrecv.at[2 + h])
        pltpu.make_async_copy(fsend2.at[h, dp], frecv2.at[h, dp], zrecv.at[2 + h]).start()

    for kind in range(3):
        if kind == 1:
            forward(kind)
        elif kind > 1:
            forward2(kind - 2)
        if kind == 0:
            copies[2].wait()
            copies[3].wait()
            prod = gv[...].astype(F32) * ov[...].astype(F32)
            hi = prod.astype(BF16)
            lo = (prod - hi.astype(F32)).astype(BF16)
            pick = (iota((8, 8 * HD), 1) // HD == iota((8, 8 * HD), 0)).astype(BF16)
            delta = (mm(pick, hi, 1, 1) + mm(pick, lo, 1, 1)).astype(BF16).astype(F32)
            for t in range(NY):
                del_s[t, 0:2, :] = delta[2 * t : 2 * t + 2, :]
                del_s[t, 2:8, :] = jnp.zeros((6, TOK), F32)
            del_r[y] = del_s[y]
            for t in ring_y:
                pltpu.make_async_remote_copy(
                    src_ref=del_s.at[t], dst_ref=del_r.at[y], send_sem=ydsend, recv_sem=ydrecv,
                    device_id=(dp, t), device_id_type=MESH,
                ).start()
        if kind == 1:
            pltpu.make_async_copy(del_r.at[pl.ds(0, NY - 1)], del_r.at[pl.ds(0, NY - 1)], ydrecv).wait()
            owner = (iota((NDP, NY * TOK), 0).astype(F32) == packs).astype(F32).astype(BF16)
            lane = iota((128, NY * TOK), 0)
            vals = [jnp.concatenate([meta_r[t, 2:3, :] for t in range(NY)], axis=1)]
            vals += [jnp.concatenate([del_r[t, j : j + 1, :] for t in range(NY)], axis=1) for j in range(2)]
            kindv = jnp.where(lane // 16 == 0, vals[0], jnp.where(lane // 16 == 1, vals[1], vals[2]))
            hit = (lax.rem(lane, 16).astype(F32) == slots) & (lane < 48)
            small = jnp.where(hit, kindv, 0.0).astype(BF16)
            msend[...] = mm(owner, small, 1, 1).reshape(NDP, 1, 128)

            everyone(msend, mrecv, zmsend, zmrecv)

    for t in range(NY):
        col = mm(eye, meta_r[t].astype(BF16), 1, 1)
        home = (col[:, 0:1] * (2.0 * SLOT) + col[:, 1:2]).astype(jnp.int32)
        for half in range(2):
            row = half * NY * TOK + t * TOK

            def gather_block(b, carry):
                r = iota((TOK, HD), 1) + b * HD
                gather[row : row + TOK, pl.ds(pl.multiple_of(b * HD, HD), HD)] = (
                    (r == home + half * SLOT).astype(F32).astype(BF16)
                )
                return carry

            lax.fori_loop(0, 2 * ROWS // HD, gather_block, 0)

    own_col = mm(eye, jnp.broadcast_to(prow, (8, TOK)).astype(BF16), 1, 1)[:, 0:1] * (2.0 * SLOT)
    own_col = (own_col + mm(eye, jnp.broadcast_to(rank, (8, TOK)).astype(BF16), 1, 1)[:, 0:1]).astype(jnp.int32)

    def kgather_block(b, carry):
        r = iota((TOK, HD), 1) + b * HD
        at = pl.ds(pl.multiple_of(b * HD, HD), HD)
        for cb in range(8):
            kgather[cb * TOK : (cb + 1) * TOK, at] = (r == own_col + CAP * cb).astype(F32).astype(BF16)
        return carry

    lax.fori_loop(0, 2 * ROWS // HD, kgather_block, 0)

    def by_head(r):
        return (lax.rem(r, 24) // 3) * 24 + (r // 48) * 6 + (lax.rem(r, 48) // 24) * 3 + lax.rem(r, 3)

    def by_ctx(r):
        return (lax.rem(r, 12) // 3) * 48 + (r // 96) * 24 + (lax.rem(r, 96) // 12) * 3 + lax.rem(r, 3)

    ia, ib = iota((192, 192), 0), iota((192, 192), 1)
    head_out = (ib == by_head(ia)).astype(F32).astype(BF16)
    head_in = (ia == by_head(ib)).astype(F32).astype(BF16)
    ctx_out = (ib == by_ctx(ia)).astype(F32).astype(BF16)
    ctx_in = (ia == by_ctx(ib)).astype(F32).astype(BF16)

    def exchange(src, dst, rsem):
        for t in ring_y:
            pltpu.make_async_remote_copy(
                src_ref=src.at[t], dst_ref=dst.at[y], send_sem=kysend, recv_sem=rsem,
                device_id=(dp, t), device_id_type=MESH,
            ).start()
        pltpu.make_async_copy(src.at[y], dst.at[y], rsem).start()

    pltpu.make_async_copy(frecv.at[0], frecv.at[0], zrecv.at[0]).wait()

    def deal(b, carry):
        got = mm(head_out, frecv[0, pl.ds(b * GRP, GRP)].reshape(192, 128), 1, 0).astype(BF16)
        at = pl.ds(pl.multiple_of(b * 48, 48), 48)
        for t in range(NY):
            ksend[t, at, :] = got[48 * t : 48 * t + 48]
        return carry

    lax.fori_loop(0, NDP // GRP, deal, 0)
    exchange(ksend, krecv, kyrecv.at[0])
    forward2(1)

    a, b = iota((192, 192), 0), iota((192, 192), 1)
    split = (b == (lax.rem(a, 96) // 12) * 24 + (a // 96) * 12 + lax.rem(a, 12)).astype(F32).astype(BF16)
    join = (a == (lax.rem(b, 96) // 12) * 24 + (b // 96) * 12 + lax.rem(b, 12)).astype(F32).astype(BF16)

    pltpu.make_async_copy(mrecv, mrecv, zmrecv).wait()
    spread = (iota((ROWS, NDP), 0) // SLOT == iota((ROWS, NDP), 1)).astype(F32).astype(BF16)
    rows = mm(spread, mrecv[...].reshape(NDP, 128).astype(BF16), 1, 0)
    r12, l128 = lax.rem(iota((ROWS, 128), 0), SLOT), iota((ROWS, 128), 1)
    own = jnp.where((lax.rem(l128, 16) == r12) & (l128 < 48), rows, 0.0)
    labcol = jnp.sum(jnp.where(l128 < 16, own, 0.0), axis=1, keepdims=True)
    labk[...] = jnp.broadcast_to(jnp.where(labcol > 0.5, labcol, -1.0), (ROWS, 128))
    pick16 = (iota((8, 128), 1) // 16 == iota((8, 128), 0)).astype(F32).astype(BF16)
    rowv[...] = mm(pick16, own.astype(BF16), 1, 1)

    def take(kind):
        pltpu.make_async_copy(frecv.at[kind], frecv.at[kind], zrecv.at[kind]).wait()

        def unmix(b, carry):
            block = frecv[kind, pl.ds(b * GRP, GRP)].reshape(192, 128)
            got = mm(split, block, 1, 0).astype(BF16)
            at = pl.ds(pl.multiple_of(b * 96, 96), 96)
            xs[kind, at, 0:128] = got[0:96]
            xs[kind, at, 128:256] = got[96:192]
            return carry

        lax.fori_loop(0, NDP // GRP, unmix, 0)

    def take2(h):
        def unmix(b, carry):
            here = pl.ds(b * GRP, GRP)
            block = jnp.concatenate(
                [frecv2[h, here, 0:3].reshape(192, 128), frecv2[h, here, 3:6].reshape(192, 128)], axis=1
            )
            got = mm(split, block, 1, 0).astype(BF16)
            at = pl.ds(pl.multiple_of(b * 96, 96), 96)
            for j in range(2):
                xs[2 + 2 * h + j, at, 0:128] = got[0:96, 128 * j : 128 * j + 128]
                xs[2 + 2 * h + j, at, 128:256] = got[96:192, 128 * j : 128 * j + 128]
            return carry

        lax.fori_loop(0, NDP // GRP, unmix, 0)

    def give(kind):
        def mix(b, carry):
            at = pl.ds(pl.multiple_of(b * 96, 96), 96)
            v = dq_acc[at, :].astype(BF16)
            got = mm(join, jnp.concatenate([v[:, 0:128], v[:, 128:256]], axis=0), 1, 0).astype(BF16)
            bsend[kind, pl.ds(b * GRP, GRP)] = got.reshape(GRP, 3, 8, 128)
            return carry

        lax.fori_loop(0, NDP // GRP, mix, 0)

    take(1)
    pltpu.make_async_copy(krecv, krecv, kyrecv.at[0]).wait()

    def collect(b, carry):
        at = pl.ds(pl.multiple_of(b * 48, 48), 48)
        got = mm(ctx_out, jnp.concatenate([krecv[t, at, :] for t in range(NY)], axis=0), 1, 0).astype(BF16)
        at = pl.ds(pl.multiple_of(b * 96, 96), 96)
        xs[0, at, 0:128] = got[0:96]
        xs[0, at, 128:256] = got[96:192]
        return carry

    lax.fori_loop(0, NDP // GRP, collect, 0)
    for g in range(2):
        if g == 1:
            for k in range(EARLY):
                spread_out(plane(1 + k), 0, bsend.at[0], brecv.at[0], bsem_s, bsem_r.at[0])
        pltpu.make_async_copy(frecv2.at[g], frecv2.at[g], zrecv.at[2 + g]).wait()
        if g == 1:
            everyone(bsend.at[0], brecv.at[0], bsem_s, bsem_r.at[0], EARLY)
        take2(g)

        def attend(b, carry):
            at = pl.ds(pl.multiple_of(b * HD, HD), HD)
            key, val = xs[0], xs[1]
            qb, gb = xs[2 + 2 * g, at, :], xs[3 + 2 * g, at, :]
            s = mm(key, qb, 1, 1) * SCALE
            ok = labk[:, 0:1] == rowv[0:1, at]
            s = jnp.where(ok, s, MASKED)
            top = jnp.max(s, axis=0, keepdims=True)
            e = jnp.exp(s - top)
            p = e * (1.0 / jnp.sum(e, axis=0, keepdims=True))
            d = mm(val, gb, 1, 1) - rowv[1 + g : 2 + g, at]
            ds = (p * d).astype(BF16)
            pv = mm(p.astype(BF16), gb, 1, 0)
            pk = mm(ds, qb, 1, 0)
            if g == 0:
                first = b == 0
                dv_acc[...] = jnp.where(first, 0.0, dv_acc[...]) + pv
                dk_acc[...] = jnp.where(first, 0.0, dk_acc[...]) + pk
            else:
                dv_acc[...] += pv
                dk_acc[...] += pk
            dq_acc[at, :] = mm(ds, key, 0, 0) * SCALE
            return carry

        if g == 0:
            dv_acc[...] = jnp.zeros((ROWS, HD), F32)
            dk_acc[...] = jnp.zeros((ROWS, HD), F32)
        lax.fori_loop(0, ROWS // HD, attend, 0)
        give(g)
    everyone(bsend.at[1], brecv.at[1], bsem_s, bsem_r.at[1])

    for n, acc in enumerate((dk_acc, dv_acc)):

        def deal_back(b, carry):
            at = pl.ds(pl.multiple_of(b * 96, 96), 96)
            v = (acc[at, :] * SCALE if n == 0 else acc[at, :]).astype(BF16)
            got = mm(ctx_in, jnp.concatenate([v[:, 0:128], v[:, 128:256]], axis=0), 1, 0).astype(BF16)
            at = pl.ds(pl.multiple_of(b * 48, 48), 48)
            for t in range(NY):
                dksend[n, t, at, :] = got[48 * t : 48 * t + 48]
            return carry

        lax.fori_loop(0, NDP // GRP, deal_back, 0)
        exchange(dksend.at[n], dkrecv.at[n], kyrecv.at[1 + n])

    def home(kind, got, ref, col, sem):
        for t in range(NY):
            obuf[kind, t, :, 0:128] = got[t * TOK : (t + 1) * TOK]
            obuf[kind, t, :, 128:256] = got[(NY + t) * TOK : (NY + t + 1) * TOK]
        cols = pl.ds(pl.multiple_of(col, HD), HD)
        for t in ring_y:
            pltpu.make_async_remote_copy(
                src_ref=obuf.at[kind, t], dst_ref=ref.at[:, cols], send_sem=osem_s, recv_sem=sem,
                device_id=(dp, t), device_id_type=MESH,
            ).start()
        pltpu.make_async_copy(obuf.at[kind, y], ref.at[:, cols], sem).start()

    def home_q(g):
        pltpu.make_async_copy(brecv.at[g], brecv.at[g], bsem_r.at[g]).wait()
        got = mm(gather[...], brecv[g].reshape(2 * ROWS, 128), 1, 0).astype(BF16)
        home(g, got, oq_ref, y * 2 * HD + g * HD, osem_r.at[0])

    home_q(0)
    for n in range(2):
        pltpu.make_async_copy(dkrecv.at[n], dkrecv.at[n], kyrecv.at[1 + n]).wait()

        def collect_back(b, carry):
            at = pl.ds(pl.multiple_of(b * 48, 48), 48)
            got = mm(head_in, jnp.concatenate([dkrecv[n, t, at, :] for t in range(NY)], axis=0), 1, 0).astype(BF16)
            bsend[2 + n, pl.ds(b * GRP, GRP)] = got.reshape(GRP, 3, 8, 128)
            return carry

        lax.fori_loop(0, NDP // GRP, collect_back, 0)
        everyone(bsend.at[2 + n], brecv.at[2 + n], bsem_s, bsem_r.at[2 + n])
    home_q(1)
    for n, ref in enumerate((ok_ref, ov_ref)):
        pltpu.make_async_copy(brecv.at[2 + n], brecv.at[2 + n], bsem_r.at[2 + n]).wait()
        got = mm(kgather[...], brecv[2 + n].reshape(2 * ROWS, 128), 1, 0).astype(BF16)
        for cb in range(8):
            kvout[n, :, cb * TOK : (cb + 1) * TOK] = got[cb * TOK : (cb + 1) * TOK]
        pltpu.make_async_copy(kvout.at[n], ref, osem_r.at[1 + n]).start()

    pltpu.make_async_copy(oq_ref, oq_ref, osem_r.at[0]).wait()
    pltpu.make_async_copy(ok_ref, ok_ref, osem_r.at[1]).wait()
    pltpu.make_async_copy(ov_ref, ov_ref, osem_r.at[2]).wait()
    some = pl.ds(0, NY - 1)
    pltpu.make_async_copy(meta_r.at[some], meta_r.at[some], ymsend).wait()
    pltpu.make_async_copy(del_r.at[some], del_r.at[some], ydsend).wait()
    pltpu.make_async_copy(tok.at[1:NT, some], tok.at[1:NT, some], ysend).wait()
    pltpu.make_async_copy(ksend.at[some], ksend.at[some], kysend).wait()
    pltpu.make_async_copy(dksend.at[:, some], dksend.at[:, some], kysend).wait()
    pltpu.make_async_copy(obuf.at[:, some], obuf.at[:, some], osem_s).wait()
    most = pl.ds(0, NDP - 1)
    pltpu.make_async_copy(msend.at[most], msend.at[most], zmsend).wait()
    pltpu.make_async_copy(fsend.at[:, most], fsend.at[:, most], zsend).wait()
    pltpu.make_async_copy(fsend2.at[:, most], fsend2.at[:, most], zsend).wait()
    pltpu.make_async_copy(bsend.at[:, most], bsend.at[:, most], bsem_s).wait()


def settle(a_ref, b_ref, c_ref, oa_ref, ob_ref, oc_ref):
    oa_ref[...] = a_ref[...]
    ob_ref[...] = b_ref[...]
    oc_ref[...] = c_ref[...]


def body(queries, key_rows, values, saved_out, out_grad, pack_of, segment_label):
    anywhere = pl.BlockSpec(memory_space=pl.ANY)
    hbm = pl.BlockSpec(memory_space=pltpu.HBM)
    dma = pltpu.SemaphoreType.DMA
    shapes = tuple(jax.ShapeDtypeStruct((TOK, n * HD), BF16) for n in (8, 4, 4))
    grads = pl.pallas_call(
        kernel,
        out_shape=shapes,
        in_specs=[hbm] * 7,
        out_specs=(anywhere,) * 3,
        scratch_shapes=[
            pltpu.VMEM((2, 1, TOK), jnp.int32),
            pltpu.VMEM((TOK, 8 * HD), BF16),
            pltpu.VMEM((TOK, 8 * HD), BF16),
            pltpu.VMEM((NT, NY, TOK, HD), BF16),
            pltpu.VMEM((8, TOK), F32),
            pltpu.VMEM((NY, 8, TOK), F32),
            pltpu.VMEM((NY, 8, TOK), F32),
            pltpu.VMEM((NY, 8, TOK), F32),
            pltpu.VMEM((2 * ROWS, 2 * NY * TOK), BF16),
            pltpu.VMEM((2 * NY * TOK, 2 * ROWS), BF16),
            pltpu.VMEM((2, NDP, 3, 8, 128), BF16),
            pltpu.VMEM((2, NDP, 3, 8, 128), BF16),
            pltpu.VMEM((NDP, 1, 128), F32),
            pltpu.VMEM((NDP, 1, 128), F32),
            pltpu.VMEM((NT, ROWS, HD), BF16),
            pltpu.VMEM((8, ROWS), F32),
            pltpu.VMEM((ROWS, 128), F32),
            pltpu.VMEM((ROWS, HD), F32),
            pltpu.VMEM((ROWS, HD), F32),
            pltpu.VMEM((ROWS, HD), F32),
            pltpu.VMEM((4, NDP, 3, 8, 128), BF16),
            pltpu.VMEM((4, NDP, 3, 8, 128), BF16),
            pltpu.VMEM((2, NY, TOK, HD), BF16),
            pltpu.VMEM((2, NDP, 6, 8, 128), BF16),
            pltpu.VMEM((2, NDP, 6, 8, 128), BF16),
            pltpu.VMEM((2, TOK, 4 * HD), BF16),
            pltpu.VMEM((TOK, 4 * HD), BF16),
            pltpu.VMEM((2 * ROWS, 8 * TOK), BF16),
            pltpu.VMEM((8 * TOK, 2 * ROWS), BF16),
            pltpu.VMEM((NY, 2 * 192, 128), BF16),
            pltpu.VMEM((NY, 2 * 192, 128), BF16),
            pltpu.VMEM((2, NY, 2 * 192, 128), BF16),
            pltpu.VMEM((2, NY, 2 * 192, 128), BF16),
            dma, dma, dma((3,)), dma((2,)), dma((2,)), dma, dma((NT,)), dma, dma, dma, dma, dma, dma((4,)), dma, dma,
            dma, dma((4,)), dma, dma((3,)),
            pltpu.SemaphoreType.REGULAR, pltpu.SemaphoreType.REGULAR,
        ],
        compiler_params=pltpu.CompilerParams(
            collective_id=0, has_side_effects=True, vmem_limit_bytes=63 << 20
        ),
        name="packed_attention_backward",
    )(
        queries, key_rows, values, out_grad, saved_out,
        pack_of.reshape(1, TOK), segment_label.reshape(1, TOK),
    )
    return pl.pallas_call(
        settle,
        out_shape=shapes,
        in_specs=[pl.BlockSpec(memory_space=pltpu.VMEM)] * 3,
        out_specs=(pl.BlockSpec(memory_space=pltpu.VMEM),) * 3,
        name="settle",
    )(*grads)


def solution(mesh):
    rows = P(("dp", "ctx"), None)
    return jax.shard_map(
        body,
        mesh=mesh,
        in_specs=(rows, rows, rows, rows, rows, rows, P(("dp", "ctx"))),
        out_specs=(rows, rows, rows),
        check_vma=False,
    )
```

```python
import jax
import jax.numpy as jnp
from jax import lax
from jax.experimental import pallas as pl
from jax.experimental.pallas import tpu as pltpu
from jax.sharding import PartitionSpec as P

MESH = pl.DeviceIdType.MESH
F32 = jnp.float32
BF16 = jnp.bfloat16

NDP = 64
NY = 4
TOK = 128
CAP = 3
HD = 256
SLOT = NY * CAP
ROWS = NDP * SLOT
GRP = 8
PLANE = 16
Z_ORDER = (0, 4, 1, 5, 2, 6, 3, 7)
EARLY = 3
MASKED = -1e30
SCALE = 1.0 / 16.0

NT = 6


def iota(shape, dim):
    return lax.broadcasted_iota(jnp.int32, shape, dim)


def mm(a, b, ca, cb):
    return lax.dot_general(a, b, (((ca,), (cb,)), ((), ())), preferred_element_type=F32)


def kernel(
    q_ref, k_ref, v_ref, g_ref, o_ref, pack_ref, lab_ref,
    oq_ref, ok_ref, ov_ref,
    ints, gv, ov, tok, meta_s, meta_r, del_s, del_r, place, gather, fsend, frecv, msend, mrecv, xs, rowv, labk,
    dq_acc, dk_acc, dv_acc, bsend, brecv, obuf, fsend2, frecv2, kvout,
    kv, kgather, ksend, krecv, dksend, dkrecv,
    ksem, kysend, kyrecv, insem, isem, ysend, yrecv, ymsend, ymrecv, ydsend, ydrecv, zsend, zrecv, zmsend, zmrecv,
    bsem_s, bsem_r, osem_s, osem_r, plane_sem, core_sem,
):
    dp = lax.axis_index("dp")
    y = lax.axis_index("ctx")
    x, z, c = dp // 16, lax.rem(dp // 2, 8), lax.rem(dp, 2)
    bar = pltpu.get_barrier_semaphore()

    copies = [
        pltpu.make_async_copy(pack_ref, ints.at[0], isem.at[0]),
        pltpu.make_async_copy(lab_ref, ints.at[1], isem.at[1]),
        pltpu.make_async_copy(g_ref, gv, insem.at[0]),
        pltpu.make_async_copy(o_ref, ov, insem.at[1]),
        pltpu.make_async_copy(k_ref, kv, ksem),
    ]
    for n in (0, 1, 4):
        copies[n].start()

    def spot(nx, nz, nc):
        return (nx * 8 + nz) * 2 + nc

    def greet(sem, d, t):
        pl.semaphore_signal(sem, inc=1, device_id=(d, t), device_id_type=MESH)

    ring_x = [spot(lax.rem(x + j, 4), z, c) for j in range(1, 4)]
    other = spot(x, z, 1 - c)
    ring_y = [lax.rem(y + j, NY) for j in range(1, NY)]
    for t in ring_y:
        greet(bar, dp, t)
    for d in ring_x:
        greet(bar, d, y)
    greet(bar, other, y)
    for j in range(1, 8):
        greet(bar, spot(x, lax.rem(z + j, 8), c), y)

    def columns(kind, head):
        if kind == 1:
            return v_ref.at[:, pl.ds(pl.multiple_of(head * HD, HD), HD)]
        ref = q_ref if kind % 2 == 0 else g_ref
        return ref.at[:, pl.ds(pl.multiple_of(head * 2 * HD + (kind // 2 - 1) * HD, HD), HD)]

    eye = (iota((TOK, TOK), 0) == iota((TOK, TOK), 1)).astype(F32).astype(BF16)
    copies[0].wait()
    copies[1].wait()
    prow = ints[0].astype(F32)
    pcol = mm(eye, jnp.broadcast_to(prow, (8, TOK)).astype(BF16), 1, 1)[:, 0:1]
    earlier = (pcol == prow) & (iota((TOK, TOK), 0) < iota((TOK, TOK), 1))
    rank = jnp.sum(earlier.astype(F32), axis=0, keepdims=True)
    slot = rank + (y * CAP).astype(F32)
    meta_s[0:1, :] = prow
    meta_s[1:2, :] = slot
    meta_s[2:3, :] = ints[1].astype(F32) + 1.0
    meta_s[3:8, :] = jnp.zeros((5, TOK), F32)
    meta_r[y] = meta_s[...]

    pl.semaphore_wait(bar, 14)

    for d in ring_x:
        greet(plane_sem, d, y)

    own_row = (prow * (2.0 * SLOT) + rank).astype(jnp.int32)

    spin = [lax.rem(dp + j, PLANE) for j in range(PLANE)]

    def plane(k):
        return lax.rem(x + k, 4)

    def spread_out(g, first, src, dst, ssem, rsem):
        for j in range(first, PLANE):
            d = g * PLANE + spin[j]
            pltpu.make_async_remote_copy(
                src_ref=src.at[d], dst_ref=dst.at[dp], send_sem=ssem, recv_sem=rsem,
                device_id=(d, y), device_id_type=MESH,
            ).start()

    def fill_k(g):
        r = iota((24 * PLANE, TOK), 0) + g * (24 * PLANE)
        hot = jnp.concatenate([(r == own_row + CAP * cb).astype(F32).astype(BF16) for cb in range(8)], axis=1)
        stack = jnp.concatenate([kv[:, cb * TOK : (cb + 1) * TOK] for cb in range(8)], axis=0)
        fsend[0, pl.ds(g * PLANE, PLANE)] = mm(hot, stack, 1, 0).astype(BF16).reshape(PLANE, 3, 8, 128)

    def step_k(k, carry):
        spread_out(plane(k), 0, fsend.at[0], frecv.at[0], zsend, zrecv.at[0])
        fill_k(plane(k + 1))
        return carry

    def columns_out(kind):
        for t in ring_y:
            pltpu.make_async_remote_copy(
                src_ref=columns(kind, t), dst_ref=tok.at[kind, y], send_sem=ysend, recv_sem=yrecv.at[kind],
                device_id=(dp, t), device_id_type=MESH,
            ).start()
        pltpu.make_async_copy(columns(kind, y), tok.at[kind, y], yrecv.at[kind]).start()

    copies[4].wait()
    fill_k(plane(1))
    pl.semaphore_wait(plane_sem, 3)
    greet(core_sem, other, y)
    for t in ring_y:
        pltpu.make_async_remote_copy(
            src_ref=meta_s, dst_ref=meta_r.at[y], send_sem=ymsend, recv_sem=ymrecv,
            device_id=(dp, t), device_id_type=MESH,
        ).start()
    columns_out(1)
    pl.semaphore_wait(core_sem, 1)
    lax.fori_loop(1, 4, step_k, 0)
    spread_out(x, 1, fsend.at[0], frecv.at[0], zsend, zrecv.at[0])
    pltpu.make_async_copy(fsend.at[0, dp], frecv.at[0, dp], zrecv.at[0]).start()
    copies[2].start()
    copies[3].start()
    for kind in range(2, NT):
        columns_out(kind)

    pltpu.make_async_copy(meta_r.at[pl.ds(0, NY - 1)], meta_r.at[pl.ds(0, NY - 1)], ymrecv).wait()
    packs = jnp.concatenate([meta_r[t, 0:1, :] for t in range(NY)], axis=1)
    slots = jnp.concatenate([meta_r[t, 1:2, :] for t in range(NY)], axis=1)
    where = (packs * (2.0 * SLOT) + slots).astype(jnp.int32)

    def place_block(b, carry):
        r = iota((HD, NY * TOK), 0) + b * HD
        at = pl.ds(pl.multiple_of(b * HD, HD), HD)
        place[at, 0 : NY * TOK] = (r == where).astype(F32).astype(BF16)
        place[at, NY * TOK : 2 * NY * TOK] = (r == where + SLOT).astype(F32).astype(BF16)
        return carry

    lax.fori_loop(0, 2 * ROWS // HD, place_block, 0)

    def everyone(src, dst, ssem, rsem, done=0):
        def send(k, carry):
            spread_out(plane(k), 0, src, dst, ssem, rsem)
            return carry

        lax.fori_loop(1 + done, 4, send, 0)
        spread_out(x, 1, src, dst, ssem, rsem)
        pltpu.make_async_copy(src.at[dp], dst.at[dp], rsem).start()

    def by_z(src, dst, ssem, rsem):
        for nz in Z_ORDER:
            for j in range(8):
                d = spot(lax.rem(x + 1 + j // 2, 4), nz, j % 2)

                @pl.when(d != dp)
                def _():
                    pltpu.make_async_remote_copy(
                        src_ref=src.at[d], dst_ref=dst.at[dp], send_sem=ssem, recv_sem=rsem,
                        device_id=(d, y), device_id_type=MESH,
                    ).start()

        pltpu.make_async_copy(src.at[dp], dst.at[dp], rsem).start()

    def landed(kind):
        pltpu.make_async_copy(tok.at[kind], tok.at[kind], yrecv.at[kind]).wait()

    def weave(kind):
        t = tok[kind].reshape(NY * TOK, HD)
        return jnp.concatenate([t[:, 0:128], t[:, 128:256]], axis=0)

    def placed(g):
        return place[pl.ds(pl.multiple_of(g * 24 * PLANE, 24 * PLANE), 24 * PLANE), :]

    def forward(kind):
        landed(kind)

        def fill(g):
            got = mm(placed(g), weave(kind), 1, 0)
            fsend[kind, pl.ds(g * PLANE, PLANE)] = got.astype(BF16).reshape(PLANE, 3, 8, 128)

        def step(k, carry):
            fill(plane(k))
            spread_out(plane(k), 0, fsend.at[kind], frecv.at[kind], zsend, zrecv.at[kind])
            return carry

        lax.fori_loop(1, 4, step, 0)
        fill(x)
        spread_out(x, 1, fsend.at[kind], frecv.at[kind], zsend, zrecv.at[kind])
        pltpu.make_async_copy(fsend.at[kind, dp], frecv.at[kind, dp], zrecv.at[kind]).start()

    def forward2(h):
        landed(2 + 2 * h)
        landed(3 + 2 * h)

        def fill(g):
            both = jnp.concatenate([weave(2 + 2 * h), weave(3 + 2 * h)], axis=1)
            got = mm(placed(g), both, 1, 0).astype(BF16)
            here = pl.ds(g * PLANE, PLANE)
            fsend2[h, here, 0:3] = got[:, 0:128].reshape(PLANE, 3, 8, 128)
            fsend2[h, here, 3:6] = got[:, 128:256].reshape(PLANE, 3, 8, 128)

        def step(k, carry):
            fill(plane(k))
            spread_out(plane(k), 0, fsend2.at[h], frecv2.at[h], zsend, zrecv.at[2 + h])
            return carry

        lax.fori_loop(1, 4, step, 0)
        fill(x)
        spread_out(x, 1, fsend2.at[h], frecv2.at[h], zsend, zrecv.at[2 + h])
        pltpu.make_async_copy(fsend2.at[h, dp], frecv2.at[h, dp], zrecv.at[2 + h]).start()

    for kind in range(3):
        if kind == 1:
            forward(kind)
        elif kind > 1:
            forward2(kind - 2)
        if kind == 0:
            copies[2].wait()
            copies[3].wait()
            prod = gv[...].astype(F32) * ov[...].astype(F32)
            hi = prod.astype(BF16)
            lo = (prod - hi.astype(F32)).astype(BF16)
            pick = (iota((8, 8 * HD), 1) // HD == iota((8, 8 * HD), 0)).astype(BF16)
            delta = (mm(pick, hi, 1, 1) + mm(pick, lo, 1, 1)).astype(BF16).astype(F32)
            for t in range(NY):
                del_s[t, 0:2, :] = delta[2 * t : 2 * t + 2, :]
                del_s[t, 2:8, :] = jnp.zeros((6, TOK), F32)
            del_r[y] = del_s[y]
            for t in ring_y:
                pltpu.make_async_remote_copy(
                    src_ref=del_s.at[t], dst_ref=del_r.at[y], send_sem=ydsend, recv_sem=ydrecv,
                    device_id=(dp, t), device_id_type=MESH,
                ).start()
        if kind == 1:
            pltpu.make_async_copy(del_r.at[pl.ds(0, NY - 1)], del_r.at[pl.ds(0, NY - 1)], ydrecv).wait()
            owner = (iota((NDP, NY * TOK), 0).astype(F32) == packs).astype(F32).astype(BF16)
            lane = iota((128, NY * TOK), 0)
            vals = [jnp.concatenate([meta_r[t, 2:3, :] for t in range(NY)], axis=1)]
            vals += [jnp.concatenate([del_r[t, j : j + 1, :] for t in range(NY)], axis=1) for j in range(2)]
            kindv = jnp.where(lane // 16 == 0, vals[0], jnp.where(lane // 16 == 1, vals[1], vals[2]))
            hit = (lax.rem(lane, 16).astype(F32) == slots) & (lane < 48)
            small = jnp.where(hit, kindv, 0.0).astype(BF16)
            msend[...] = mm(owner, small, 1, 1).reshape(NDP, 1, 128)

            everyone(msend, mrecv, zmsend, zmrecv)

    for t in range(NY):
        col = mm(eye, meta_r[t].astype(BF16), 1, 1)
        home = (col[:, 0:1] * (2.0 * SLOT) + col[:, 1:2]).astype(jnp.int32)
        for half in range(2):
            row = half * NY * TOK + t * TOK

            def gather_block(b, carry):
                r = iota((TOK, HD), 1) + b * HD
                gather[row : row + TOK, pl.ds(pl.multiple_of(b * HD, HD), HD)] = (
                    (r == home + half * SLOT).astype(F32).astype(BF16)
                )
                return carry

            lax.fori_loop(0, 2 * ROWS // HD, gather_block, 0)

    own_col = mm(eye, jnp.broadcast_to(prow, (8, TOK)).astype(BF16), 1, 1)[:, 0:1] * (2.0 * SLOT)
    own_col = (own_col + mm(eye, jnp.broadcast_to(rank, (8, TOK)).astype(BF16), 1, 1)[:, 0:1]).astype(jnp.int32)

    def kgather_block(b, carry):
        r = iota((TOK, HD), 1) + b * HD
        at = pl.ds(pl.multiple_of(b * HD, HD), HD)
        for cb in range(8):
            kgather[cb * TOK : (cb + 1) * TOK, at] = (r == own_col + CAP * cb).astype(F32).astype(BF16)
        return carry

    lax.fori_loop(0, 2 * ROWS // HD, kgather_block, 0)

    def by_head(r):
        return (lax.rem(r, 24) // 3) * 24 + (r // 48) * 6 + (lax.rem(r, 48) // 24) * 3 + lax.rem(r, 3)

    def by_ctx(r):
        return (lax.rem(r, 12) // 3) * 48 + (r // 96) * 24 + (lax.rem(r, 96) // 12) * 3 + lax.rem(r, 3)

    ia, ib = iota((192, 192), 0), iota((192, 192), 1)
    head_out = (ib == by_head(ia)).astype(F32).astype(BF16)
    head_in = (ia == by_head(ib)).astype(F32).astype(BF16)
    ctx_out = (ib == by_ctx(ia)).astype(F32).astype(BF16)
    ctx_in = (ia == by_ctx(ib)).astype(F32).astype(BF16)

    def exchange(src, dst, rsem):
        for t in ring_y:
            pltpu.make_async_remote_copy(
                src_ref=src.at[t], dst_ref=dst.at[y], send_sem=kysend, recv_sem=rsem,
                device_id=(dp, t), device_id_type=MESH,
            ).start()
        pltpu.make_async_copy(src.at[y], dst.at[y], rsem).start()

    pltpu.make_async_copy(frecv.at[0], frecv.at[0], zrecv.at[0]).wait()

    def deal(b, carry):
        got = mm(head_out, frecv[0, pl.ds(b * GRP, GRP)].reshape(192, 128), 1, 0).astype(BF16)
        at = pl.ds(pl.multiple_of(b * 48, 48), 48)
        for t in range(NY):
            ksend[t, at, :] = got[48 * t : 48 * t + 48]
        return carry

    lax.fori_loop(0, NDP // GRP, deal, 0)
    exchange(ksend, krecv, kyrecv.at[0])
    forward2(1)

    a, b = iota((192, 192), 0), iota((192, 192), 1)
    split = (b == (lax.rem(a, 96) // 12) * 24 + (a // 96) * 12 + lax.rem(a, 12)).astype(F32).astype(BF16)
    join = (a == (lax.rem(b, 96) // 12) * 24 + (b // 96) * 12 + lax.rem(b, 12)).astype(F32).astype(BF16)

    pltpu.make_async_copy(mrecv, mrecv, zmrecv).wait()
    spread = (iota((ROWS, NDP), 0) // SLOT == iota((ROWS, NDP), 1)).astype(F32).astype(BF16)
    rows = mm(spread, mrecv[...].reshape(NDP, 128).astype(BF16), 1, 0)
    r12, l128 = lax.rem(iota((ROWS, 128), 0), SLOT), iota((ROWS, 128), 1)
    own = jnp.where((lax.rem(l128, 16) == r12) & (l128 < 48), rows, 0.0)
    labcol = jnp.sum(jnp.where(l128 < 16, own, 0.0), axis=1, keepdims=True)
    labk[...] = jnp.broadcast_to(jnp.where(labcol > 0.5, labcol, -1.0), (ROWS, 128))
    pick16 = (iota((8, 128), 1) // 16 == iota((8, 128), 0)).astype(F32).astype(BF16)
    rowv[...] = mm(pick16, own.astype(BF16), 1, 1)

    def take(kind):
        pltpu.make_async_copy(frecv.at[kind], frecv.at[kind], zrecv.at[kind]).wait()

        def unmix(b, carry):
            block = frecv[kind, pl.ds(b * GRP, GRP)].reshape(192, 128)
            got = mm(split, block, 1, 0).astype(BF16)
            at = pl.ds(pl.multiple_of(b * 96, 96), 96)
            xs[kind, at, 0:128] = got[0:96]
            xs[kind, at, 128:256] = got[96:192]
            return carry

        lax.fori_loop(0, NDP // GRP, unmix, 0)

    def take2(h):
        def unmix(b, carry):
            here = pl.ds(b * GRP, GRP)
            block = jnp.concatenate(
                [frecv2[h, here, 0:3].reshape(192, 128), frecv2[h, here, 3:6].reshape(192, 128)], axis=1
            )
            got = mm(split, block, 1, 0).astype(BF16)
            at = pl.ds(pl.multiple_of(b * 96, 96), 96)
            for j in range(2):
                xs[2 + 2 * h + j, at, 0:128] = got[0:96, 128 * j : 128 * j + 128]
                xs[2 + 2 * h + j, at, 128:256] = got[96:192, 128 * j : 128 * j + 128]
            return carry

        lax.fori_loop(0, NDP // GRP, unmix, 0)

    def give(kind):
        def mix(b, carry):
            at = pl.ds(pl.multiple_of(b * 96, 96), 96)
            v = dq_acc[at, :].astype(BF16)
            got = mm(join, jnp.concatenate([v[:, 0:128], v[:, 128:256]], axis=0), 1, 0).astype(BF16)
            bsend[kind, pl.ds(b * GRP, GRP)] = got.reshape(GRP, 3, 8, 128)
            return carry

        lax.fori_loop(0, NDP // GRP, mix, 0)

    take(1)
    pltpu.make_async_copy(krecv, krecv, kyrecv.at[0]).wait()

    def collect(b, carry):
        at = pl.ds(pl.multiple_of(b * 48, 48), 48)
        got = mm(ctx_out, jnp.concatenate([krecv[t, at, :] for t in range(NY)], axis=0), 1, 0).astype(BF16)
        at = pl.ds(pl.multiple_of(b * 96, 96), 96)
        xs[0, at, 0:128] = got[0:96]
        xs[0, at, 128:256] = got[96:192]
        return carry

    lax.fori_loop(0, NDP // GRP, collect, 0)
    for g in range(2):
        if g == 1:
            for k in range(EARLY):
                spread_out(plane(1 + k), 0, bsend.at[0], brecv.at[0], bsem_s, bsem_r.at[0])
        pltpu.make_async_copy(frecv2.at[g], frecv2.at[g], zrecv.at[2 + g]).wait()
        if g == 1:
            everyone(bsend.at[0], brecv.at[0], bsem_s, bsem_r.at[0], EARLY)
        take2(g)

        def attend(b, carry):
            at = pl.ds(pl.multiple_of(b * HD, HD), HD)
            key, val = xs[0], xs[1]
            qb, gb = xs[2 + 2 * g, at, :], xs[3 + 2 * g, at, :]
            s = mm(key, qb, 1, 1) * SCALE
            ok = labk[:, 0:1] == rowv[0:1, at]
            s = jnp.where(ok, s, MASKED)
            top = jnp.max(s, axis=0, keepdims=True)
            e = jnp.exp(s - top)
            p = e * (1.0 / jnp.sum(e, axis=0, keepdims=True))
            d = mm(val, gb, 1, 1) - rowv[1 + g : 2 + g, at]
            ds = (p * d).astype(BF16)
            pv = mm(p.astype(BF16), gb, 1, 0)
            pk = mm(ds, qb, 1, 0)
            if g == 0:
                first = b == 0
                dv_acc[...] = jnp.where(first, 0.0, dv_acc[...]) + pv
                dk_acc[...] = jnp.where(first, 0.0, dk_acc[...]) + pk
            else:
                dv_acc[...] += pv
                dk_acc[...] += pk
            dq_acc[at, :] = mm(ds, key, 0, 0) * SCALE
            return carry

        if g == 0:
            dv_acc[...] = jnp.zeros((ROWS, HD), F32)
            dk_acc[...] = jnp.zeros((ROWS, HD), F32)
        lax.fori_loop(0, ROWS // HD, attend, 0)
        if g == 0:
            give(0)

    def deal_out(n, acc):
        def deal_back(b, carry):
            at = pl.ds(pl.multiple_of(b * 96, 96), 96)
            v = (acc[at, :] * SCALE if n == 0 else acc[at, :]).astype(BF16)
            got = mm(ctx_in, jnp.concatenate([v[:, 0:128], v[:, 128:256]], axis=0), 1, 0).astype(BF16)
            at = pl.ds(pl.multiple_of(b * 48, 48), 48)
            for t in range(NY):
                dksend[n, t, at, :] = got[48 * t : 48 * t + 48]
            return carry

        lax.fori_loop(0, NDP // GRP, deal_back, 0)
        exchange(dksend.at[n], dkrecv.at[n], kyrecv.at[1 + n])

    deal_out(0, dk_acc)
    give(1)
    everyone(bsend.at[1], brecv.at[1], bsem_s, bsem_r.at[1])
    deal_out(1, dv_acc)

    def home(kind, got, ref, col, sem):
        for t in range(NY):
            obuf[kind, t, :, 0:128] = got[t * TOK : (t + 1) * TOK]
            obuf[kind, t, :, 128:256] = got[(NY + t) * TOK : (NY + t + 1) * TOK]
        cols = pl.ds(pl.multiple_of(col, HD), HD)
        for t in ring_y:
            pltpu.make_async_remote_copy(
                src_ref=obuf.at[kind, t], dst_ref=ref.at[:, cols], send_sem=osem_s, recv_sem=sem,
                device_id=(dp, t), device_id_type=MESH,
            ).start()
        pltpu.make_async_copy(obuf.at[kind, y], ref.at[:, cols], sem).start()

    def home_q(g):
        pltpu.make_async_copy(brecv.at[g], brecv.at[g], bsem_r.at[g]).wait()
        got = mm(gather[...], brecv[g].reshape(2 * ROWS, 128), 1, 0).astype(BF16)
        home(g, got, oq_ref, y * 2 * HD + g * HD, osem_r.at[0])

    for n in range(2):
        pltpu.make_async_copy(dkrecv.at[n], dkrecv.at[n], kyrecv.at[1 + n]).wait()

        def collect_back(b, carry):
            at = pl.ds(pl.multiple_of(b * 48, 48), 48)
            got = mm(head_in, jnp.concatenate([dkrecv[n, t, at, :] for t in range(NY)], axis=0), 1, 0).astype(BF16)
            bsend[2 + n, pl.ds(b * GRP, GRP)] = got.reshape(GRP, 3, 8, 128)
            return carry

        lax.fori_loop(0, NDP // GRP, collect_back, 0)
        by_z(bsend.at[2 + n], brecv.at[2 + n], bsem_s, bsem_r.at[2 + n])
        home_q(n)
    for n, ref in enumerate((ok_ref, ov_ref)):
        pltpu.make_async_copy(brecv.at[2 + n], brecv.at[2 + n], bsem_r.at[2 + n]).wait()
        got = mm(kgather[...], brecv[2 + n].reshape(2 * ROWS, 128), 1, 0).astype(BF16)
        for cb in range(8):
            kvout[n, :, cb * TOK : (cb + 1) * TOK] = got[cb * TOK : (cb + 1) * TOK]
        pltpu.make_async_copy(kvout.at[n], ref, osem_r.at[1 + n]).start()

    pltpu.make_async_copy(oq_ref, oq_ref, osem_r.at[0]).wait()
    pltpu.make_async_copy(ok_ref, ok_ref, osem_r.at[1]).wait()
    pltpu.make_async_copy(ov_ref, ov_ref, osem_r.at[2]).wait()
    some = pl.ds(0, NY - 1)
    pltpu.make_async_copy(meta_r.at[some], meta_r.at[some], ymsend).wait()
    pltpu.make_async_copy(del_r.at[some], del_r.at[some], ydsend).wait()
    pltpu.make_async_copy(tok.at[1:NT, some], tok.at[1:NT, some], ysend).wait()
    pltpu.make_async_copy(ksend.at[some], ksend.at[some], kysend).wait()
    pltpu.make_async_copy(dksend.at[:, some], dksend.at[:, some], kysend).wait()
    pltpu.make_async_copy(obuf.at[:, some], obuf.at[:, some], osem_s).wait()
    most = pl.ds(0, NDP - 1)
    pltpu.make_async_copy(msend.at[most], msend.at[most], zmsend).wait()
    pltpu.make_async_copy(fsend.at[:, most], fsend.at[:, most], zsend).wait()
    pltpu.make_async_copy(fsend2.at[:, most], fsend2.at[:, most], zsend).wait()
    pltpu.make_async_copy(bsend.at[:, most], bsend.at[:, most], bsem_s).wait()


def settle(a_ref, b_ref, c_ref, oa_ref, ob_ref, oc_ref, va, vb, vc, sin, sout):
    ways = ((a_ref, va, oa_ref), (b_ref, vb, ob_ref), (c_ref, vc, oc_ref))
    come = [pltpu.make_async_copy(src, mid, sin.at[n]) for n, (src, mid, _) in enumerate(ways)]
    go = [pltpu.make_async_copy(mid, dst, sout.at[n]) for n, (_, mid, dst) in enumerate(ways)]
    for copy in come:
        copy.start()
    for n in range(3):
        come[n].wait()
        go[n].start()
    for copy in go:
        copy.wait()


def body(queries, key_rows, values, saved_out, out_grad, pack_of, segment_label):
    anywhere = pl.BlockSpec(memory_space=pl.ANY)
    hbm = pl.BlockSpec(memory_space=pltpu.HBM)
    dma = pltpu.SemaphoreType.DMA
    shapes = tuple(jax.ShapeDtypeStruct((TOK, n * HD), BF16) for n in (8, 4, 4))
    grads = pl.pallas_call(
        kernel,
        out_shape=shapes,
        in_specs=[hbm] * 7,
        out_specs=(anywhere,) * 3,
        scratch_shapes=[
            pltpu.VMEM((2, 1, TOK), jnp.int32),
            pltpu.VMEM((TOK, 8 * HD), BF16),
            pltpu.VMEM((TOK, 8 * HD), BF16),
            pltpu.VMEM((NT, NY, TOK, HD), BF16),
            pltpu.VMEM((8, TOK), F32),
            pltpu.VMEM((NY, 8, TOK), F32),
            pltpu.VMEM((NY, 8, TOK), F32),
            pltpu.VMEM((NY, 8, TOK), F32),
            pltpu.VMEM((2 * ROWS, 2 * NY * TOK), BF16),
            pltpu.VMEM((2 * NY * TOK, 2 * ROWS), BF16),
            pltpu.VMEM((2, NDP, 3, 8, 128), BF16),
            pltpu.VMEM((2, NDP, 3, 8, 128), BF16),
            pltpu.VMEM((NDP, 1, 128), F32),
            pltpu.VMEM((NDP, 1, 128), F32),
            pltpu.VMEM((NT, ROWS, HD), BF16),
            pltpu.VMEM((8, ROWS), F32),
            pltpu.VMEM((ROWS, 128), F32),
            pltpu.VMEM((ROWS, HD), F32),
            pltpu.VMEM((ROWS, HD), F32),
            pltpu.VMEM((ROWS, HD), F32),
            pltpu.VMEM((4, NDP, 3, 8, 128), BF16),
            pltpu.VMEM((4, NDP, 3, 8, 128), BF16),
            pltpu.VMEM((2, NY, TOK, HD), BF16),
            pltpu.VMEM((2, NDP, 6, 8, 128), BF16),
            pltpu.VMEM((2, NDP, 6, 8, 128), BF16),
            pltpu.VMEM((2, TOK, 4 * HD), BF16),
            pltpu.VMEM((TOK, 4 * HD), BF16),
            pltpu.VMEM((8 * TOK, 2 * ROWS), BF16),
            pltpu.VMEM((NY, 2 * 192, 128), BF16),
            pltpu.VMEM((NY, 2 * 192, 128), BF16),
            pltpu.VMEM((2, NY, 2 * 192, 128), BF16),
            pltpu.VMEM((2, NY, 2 * 192, 128), BF16),
            dma, dma, dma((3,)), dma((2,)), dma((2,)), dma, dma((NT,)), dma, dma, dma, dma, dma, dma((4,)), dma, dma,
            dma, dma((4,)), dma, dma((3,)),
            pltpu.SemaphoreType.REGULAR, pltpu.SemaphoreType.REGULAR,
        ],
        compiler_params=pltpu.CompilerParams(
            collective_id=0, has_side_effects=True, vmem_limit_bytes=63 << 20
        ),
        name="packed_attention_backward",
    )(
        queries, key_rows, values, out_grad, saved_out,
        pack_of.reshape(1, TOK), segment_label.reshape(1, TOK),
    )
    return pl.pallas_call(
        settle,
        out_shape=shapes,
        in_specs=[anywhere] * 3,
        out_specs=(anywhere,) * 3,
        scratch_shapes=[pltpu.VMEM(shape.shape, BF16) for shape in shapes] + [dma((3,)), dma((3,))],
        name="settle",
    )(*grads)


def solution(mesh):
    rows = P(("dp", "ctx"), None)
    return jax.shard_map(
        body,
        mesh=mesh,
        in_specs=(rows, rows, rows, rows, rows, rows, P(("dp", "ctx"))),
        out_specs=(rows, rows, rows),
        check_vma=False,
    )
```

```python
import jax
import jax.numpy as jnp
from jax import lax
from jax.experimental import pallas as pl
from jax.experimental.pallas import tpu as pltpu
from jax.sharding import PartitionSpec as P

MESH = pl.DeviceIdType.MESH
F32 = jnp.float32
BF16 = jnp.bfloat16

NDP = 64
NY = 4
TOK = 128
CAP = 3
HD = 256
SLOT = NY * CAP
ROWS = NDP * SLOT
GRP = 8
PLANE = 16
Z_ORDER = (0, 4, 1, 5, 2, 6, 3, 7)
EARLY = 3
MASKED = -1e30
SCALE = 1.0 / 16.0

NT = 6


def iota(shape, dim):
    return lax.broadcasted_iota(jnp.int32, shape, dim)


def mm(a, b, ca, cb):
    return lax.dot_general(a, b, (((ca,), (cb,)), ((), ())), preferred_element_type=F32)


def kernel(
    q_ref, k_ref, v_ref, g_ref, o_ref, pack_ref, lab_ref,
    oq_ref, ok_ref, ov_ref,
    ints, gv, ov, tok, meta_s, meta_r, del_s, del_r, place, gather, fsend, frecv, msend, mrecv, xs, rowv, labk,
    dq_acc, dk_acc, dv_acc, bsend, brecv, obuf, fsend2, frecv2, kvout,
    kv, kgather, ksend, krecv, dksend, dkrecv,
    ksem, kysend, kyrecv, insem, isem, ysend, yrecv, ymsend, ymrecv, ydsend, ydrecv, zsend, zrecv, zmsend, zmrecv,
    bsem_s, bsem_r, osem_s, osem_r, plane_sem, core_sem,
):
    dp = lax.axis_index("dp")
    y = lax.axis_index("ctx")
    x, z, c = dp // 16, lax.rem(dp // 2, 8), lax.rem(dp, 2)
    bar = pltpu.get_barrier_semaphore()

    copies = [
        pltpu.make_async_copy(pack_ref, ints.at[0], isem.at[0]),
        pltpu.make_async_copy(lab_ref, ints.at[1], isem.at[1]),
        pltpu.make_async_copy(g_ref, gv, insem.at[0]),
        pltpu.make_async_copy(o_ref, ov, insem.at[1]),
        pltpu.make_async_copy(k_ref, kv, ksem),
    ]
    for n in (0, 1, 4):
        copies[n].start()

    def spot(nx, nz, nc):
        return (nx * 8 + nz) * 2 + nc

    def greet(sem, d, t):
        pl.semaphore_signal(sem, inc=1, device_id=(d, t), device_id_type=MESH)

    ring_x = [spot(lax.rem(x + j, 4), z, c) for j in range(1, 4)]
    other = spot(x, z, 1 - c)
    ring_y = [lax.rem(y + j, NY) for j in range(1, NY)]
    for t in ring_y:
        greet(bar, dp, t)
    for d in ring_x:
        greet(bar, d, y)
    greet(bar, other, y)
    for j in range(1, 8):
        greet(bar, spot(x, lax.rem(z + j, 8), c), y)

    def columns(kind, head):
        if kind == 1:
            return v_ref.at[:, pl.ds(pl.multiple_of(head * HD, HD), HD)]
        ref = q_ref if kind % 2 == 0 else g_ref
        return ref.at[:, pl.ds(pl.multiple_of(head * 2 * HD + (kind // 2 - 1) * HD, HD), HD)]

    eye = (iota((TOK, TOK), 0) == iota((TOK, TOK), 1)).astype(F32).astype(BF16)
    copies[0].wait()
    copies[1].wait()
    prow = ints[0].astype(F32)
    pcol = mm(eye, jnp.broadcast_to(prow, (8, TOK)).astype(BF16), 1, 1)[:, 0:1]
    earlier = (pcol == prow) & (iota((TOK, TOK), 0) < iota((TOK, TOK), 1))
    rank = jnp.sum(earlier.astype(F32), axis=0, keepdims=True)
    slot = rank + (y * CAP).astype(F32)
    meta_s[0:1, :] = prow
    meta_s[1:2, :] = slot
    meta_s[2:3, :] = ints[1].astype(F32) + 1.0
    meta_s[3:8, :] = jnp.zeros((5, TOK), F32)
    meta_r[y] = meta_s[...]

    pl.semaphore_wait(bar, 14)

    for d in ring_x:
        greet(plane_sem, d, y)

    own_row = (prow * (2.0 * SLOT) + rank).astype(jnp.int32)

    spin = [lax.rem(dp + j, PLANE) for j in range(PLANE)]

    def plane(k):
        return lax.rem(x + k, 4)

    def spread_out(g, first, src, dst, ssem, rsem):
        for j in range(first, PLANE):
            d = g * PLANE + spin[j]
            pltpu.make_async_remote_copy(
                src_ref=src.at[d], dst_ref=dst.at[dp], send_sem=ssem, recv_sem=rsem,
                device_id=(d, y), device_id_type=MESH,
            ).start()

    def fill_k(g):
        r = iota((24 * PLANE, TOK), 0) + g * (24 * PLANE)
        hot = jnp.concatenate([(r == own_row + CAP * cb).astype(F32).astype(BF16) for cb in range(8)], axis=1)
        stack = jnp.concatenate([kv[:, cb * TOK : (cb + 1) * TOK] for cb in range(8)], axis=0)
        fsend[0, pl.ds(g * PLANE, PLANE)] = mm(hot, stack, 1, 0).astype(BF16).reshape(PLANE, 3, 8, 128)

    def step_k(k, carry):
        spread_out(plane(k), 0, fsend.at[0], frecv.at[0], zsend, zrecv.at[0])
        fill_k(plane(k + 1))
        return carry

    def columns_out(kind):
        for t in ring_y:
            pltpu.make_async_remote_copy(
                src_ref=columns(kind, t), dst_ref=tok.at[kind, y], send_sem=ysend, recv_sem=yrecv.at[kind],
                device_id=(dp, t), device_id_type=MESH,
            ).start()
        pltpu.make_async_copy(columns(kind, y), tok.at[kind, y], yrecv.at[kind]).start()

    copies[4].wait()
    fill_k(plane(1))
    pl.semaphore_wait(plane_sem, 3)
    greet(core_sem, other, y)
    for t in ring_y:
        pltpu.make_async_remote_copy(
            src_ref=meta_s, dst_ref=meta_r.at[y], send_sem=ymsend, recv_sem=ymrecv,
            device_id=(dp, t), device_id_type=MESH,
        ).start()
    columns_out(1)
    pl.semaphore_wait(core_sem, 1)
    lax.fori_loop(1, 4, step_k, 0)
    spread_out(x, 1, fsend.at[0], frecv.at[0], zsend, zrecv.at[0])
    pltpu.make_async_copy(fsend.at[0, dp], frecv.at[0, dp], zrecv.at[0]).start()
    copies[2].start()
    copies[3].start()
    for kind in range(2, NT):
        columns_out(kind)

    pltpu.make_async_copy(meta_r.at[pl.ds(0, NY - 1)], meta_r.at[pl.ds(0, NY - 1)], ymrecv).wait()
    packs = jnp.concatenate([meta_r[t, 0:1, :] for t in range(NY)], axis=1)
    slots = jnp.concatenate([meta_r[t, 1:2, :] for t in range(NY)], axis=1)
    where = (packs * (2.0 * SLOT) + slots).astype(jnp.int32)

    def place_block(b, carry):
        r = iota((HD, NY * TOK), 0) + b * HD
        at = pl.ds(pl.multiple_of(b * HD, HD), HD)
        place[at, 0 : NY * TOK] = (r == where).astype(F32).astype(BF16)
        place[at, NY * TOK : 2 * NY * TOK] = (r == where + SLOT).astype(F32).astype(BF16)
        return carry

    lax.fori_loop(0, 2 * ROWS // HD, place_block, 0)

    def everyone(src, dst, ssem, rsem, done=0):
        def send(k, carry):
            spread_out(plane(k), 0, src, dst, ssem, rsem)
            return carry

        lax.fori_loop(1 + done, 4, send, 0)
        spread_out(x, 1, src, dst, ssem, rsem)
        pltpu.make_async_copy(src.at[dp], dst.at[dp], rsem).start()

    def by_z(src, dst, ssem, rsem):
        for nz in Z_ORDER:
            for j in range(8):
                d = spot(lax.rem(x + 1 + j // 2, 4), nz, j % 2)

                @pl.when(d != dp)
                def _():
                    pltpu.make_async_remote_copy(
                        src_ref=src.at[d], dst_ref=dst.at[dp], send_sem=ssem, recv_sem=rsem,
                        device_id=(d, y), device_id_type=MESH,
                    ).start()

        pltpu.make_async_copy(src.at[dp], dst.at[dp], rsem).start()

    def landed(kind):
        pltpu.make_async_copy(tok.at[kind], tok.at[kind], yrecv.at[kind]).wait()

    def weave(kind):
        t = tok[kind].reshape(NY * TOK, HD)
        return jnp.concatenate([t[:, 0:128], t[:, 128:256]], axis=0)

    def placed(g):
        return place[pl.ds(pl.multiple_of(g * 24 * PLANE, 24 * PLANE), 24 * PLANE), :]

    def forward(kind):
        landed(kind)

        def fill(g):
            got = mm(placed(g), weave(kind), 1, 0)
            fsend[kind, pl.ds(g * PLANE, PLANE)] = got.astype(BF16).reshape(PLANE, 3, 8, 128)

        def step(k, carry):
            fill(plane(k))
            spread_out(plane(k), 0, fsend.at[kind], frecv.at[kind], zsend, zrecv.at[kind])
            return carry

        lax.fori_loop(1, 4, step, 0)
        fill(x)
        spread_out(x, 1, fsend.at[kind], frecv.at[kind], zsend, zrecv.at[kind])
        pltpu.make_async_copy(fsend.at[kind, dp], frecv.at[kind, dp], zrecv.at[kind]).start()

    def forward2(h):
        landed(2 + 2 * h)
        landed(3 + 2 * h)

        def fill(g):
            both = jnp.concatenate([weave(2 + 2 * h), weave(3 + 2 * h)], axis=1)
            got = mm(placed(g), both, 1, 0).astype(BF16)
            here = pl.ds(g * PLANE, PLANE)
            fsend2[h, here, 0:3] = got[:, 0:128].reshape(PLANE, 3, 8, 128)
            fsend2[h, here, 3:6] = got[:, 128:256].reshape(PLANE, 3, 8, 128)

        def step(k, carry):
            fill(plane(k))
            spread_out(plane(k), 0, fsend2.at[h], frecv2.at[h], zsend, zrecv.at[2 + h])
            return carry

        lax.fori_loop(1, 4, step, 0)
        fill(x)
        spread_out(x, 1, fsend2.at[h], frecv2.at[h], zsend, zrecv.at[2 + h])
        pltpu.make_async_copy(fsend2.at[h, dp], frecv2.at[h, dp], zrecv.at[2 + h]).start()

    for kind in range(3):
        if kind == 1:
            forward(kind)
        elif kind > 1:
            forward2(kind - 2)
        if kind == 0:
            copies[2].wait()
            copies[3].wait()
            prod = gv[...].astype(F32) * ov[...].astype(F32)
            hi = prod.astype(BF16)
            lo = (prod - hi.astype(F32)).astype(BF16)
            pick = (iota((8, 8 * HD), 1) // HD == iota((8, 8 * HD), 0)).astype(BF16)
            delta = (mm(pick, hi, 1, 1) + mm(pick, lo, 1, 1)).astype(BF16).astype(F32)
            for t in range(NY):
                del_s[t, 0:2, :] = delta[2 * t : 2 * t + 2, :]
                del_s[t, 2:8, :] = jnp.zeros((6, TOK), F32)
            del_r[y] = del_s[y]
            for t in ring_y:
                pltpu.make_async_remote_copy(
                    src_ref=del_s.at[t], dst_ref=del_r.at[y], send_sem=ydsend, recv_sem=ydrecv,
                    device_id=(dp, t), device_id_type=MESH,
                ).start()
        if kind == 1:
            pltpu.make_async_copy(del_r.at[pl.ds(0, NY - 1)], del_r.at[pl.ds(0, NY - 1)], ydrecv).wait()
            owner = (iota((NDP, NY * TOK), 0).astype(F32) == packs).astype(F32).astype(BF16)
            lane = iota((128, NY * TOK), 0)
            vals = [jnp.concatenate([meta_r[t, 2:3, :] for t in range(NY)], axis=1)]
            vals += [jnp.concatenate([del_r[t, j : j + 1, :] for t in range(NY)], axis=1) for j in range(2)]
            kindv = jnp.where(lane // 16 == 0, vals[0], jnp.where(lane // 16 == 1, vals[1], vals[2]))
            hit = (lax.rem(lane, 16).astype(F32) == slots) & (lane < 48)
            small = jnp.where(hit, kindv, 0.0).astype(BF16)
            msend[...] = mm(owner, small, 1, 1).reshape(NDP, 1, 128)

            everyone(msend, mrecv, zmsend, zmrecv)

    for t in range(NY):
        col = mm(eye, meta_r[t].astype(BF16), 1, 1)
        home = (col[:, 0:1] * (2.0 * SLOT) + col[:, 1:2]).astype(jnp.int32)
        for half in range(2):
            row = half * NY * TOK + t * TOK

            def gather_block(b, carry):
                r = iota((TOK, HD), 1) + b * HD
                gather[row : row + TOK, pl.ds(pl.multiple_of(b * HD, HD), HD)] = (
                    (r == home + half * SLOT).astype(F32).astype(BF16)
                )
                return carry

            lax.fori_loop(0, 2 * ROWS // HD, gather_block, 0)

    own_col = mm(eye, jnp.broadcast_to(prow, (8, TOK)).astype(BF16), 1, 1)[:, 0:1] * (2.0 * SLOT)
    own_col = (own_col + mm(eye, jnp.broadcast_to(rank, (8, TOK)).astype(BF16), 1, 1)[:, 0:1]).astype(jnp.int32)

    def kgather_block(b, carry):
        r = iota((TOK, HD), 1) + b * HD
        at = pl.ds(pl.multiple_of(b * HD, HD), HD)
        for cb in range(8):
            kgather[cb * TOK : (cb + 1) * TOK, at] = (r == own_col + CAP * cb).astype(F32).astype(BF16)
        return carry

    lax.fori_loop(0, 2 * ROWS // HD, kgather_block, 0)

    def by_head(r):
        return (lax.rem(r, 24) // 3) * 24 + (r // 48) * 6 + (lax.rem(r, 48) // 24) * 3 + lax.rem(r, 3)

    def by_ctx(r):
        return (lax.rem(r, 12) // 3) * 48 + (r // 96) * 24 + (lax.rem(r, 96) // 12) * 3 + lax.rem(r, 3)

    ia, ib = iota((192, 192), 0), iota((192, 192), 1)
    head_out = (ib == by_head(ia)).astype(F32).astype(BF16)
    head_in = (ia == by_head(ib)).astype(F32).astype(BF16)
    ctx_out = (ib == by_ctx(ia)).astype(F32).astype(BF16)
    ctx_in = (ia == by_ctx(ib)).astype(F32).astype(BF16)

    def exchange(src, dst, rsem):
        for t in ring_y:
            pltpu.make_async_remote_copy(
                src_ref=src.at[t], dst_ref=dst.at[y], send_sem=kysend, recv_sem=rsem,
                device_id=(dp, t), device_id_type=MESH,
            ).start()
        pltpu.make_async_copy(src.at[y], dst.at[y], rsem).start()

    pltpu.make_async_copy(frecv.at[0], frecv.at[0], zrecv.at[0]).wait()

    def deal(b, carry):
        got = mm(head_out, frecv[0, pl.ds(b * GRP, GRP)].reshape(192, 128), 1, 0).astype(BF16)
        at = pl.ds(pl.multiple_of(b * 48, 48), 48)
        for t in range(NY):
            ksend[t, at, :] = got[48 * t : 48 * t + 48]
        return carry

    lax.fori_loop(0, NDP // GRP, deal, 0)
    exchange(ksend, krecv, kyrecv.at[0])
    forward2(1)

    a, b = iota((192, 192), 0), iota((192, 192), 1)
    split = (b == (lax.rem(a, 96) // 12) * 24 + (a // 96) * 12 + lax.rem(a, 12)).astype(F32).astype(BF16)
    join = (a == (lax.rem(b, 96) // 12) * 24 + (b // 96) * 12 + lax.rem(b, 12)).astype(F32).astype(BF16)

    pltpu.make_async_copy(mrecv, mrecv, zmrecv).wait()
    spread = (iota((ROWS, NDP), 0) // SLOT == iota((ROWS, NDP), 1)).astype(F32).astype(BF16)
    rows = mm(spread, mrecv[...].reshape(NDP, 128).astype(BF16), 1, 0)
    r12, l128 = lax.rem(iota((ROWS, 128), 0), SLOT), iota((ROWS, 128), 1)
    own = jnp.where((lax.rem(l128, 16) == r12) & (l128 < 48), rows, 0.0)
    labcol = jnp.sum(jnp.where(l128 < 16, own, 0.0), axis=1, keepdims=True)
    labk[...] = jnp.broadcast_to(jnp.where(labcol > 0.5, labcol, -1.0), (ROWS, 128))
    pick16 = (iota((8, 128), 1) // 16 == iota((8, 128), 0)).astype(F32).astype(BF16)
    rowv[...] = mm(pick16, own.astype(BF16), 1, 1)

    def take(kind):
        pltpu.make_async_copy(frecv.at[kind], frecv.at[kind], zrecv.at[kind]).wait()

        def unmix(b, carry):
            block = frecv[kind, pl.ds(b * GRP, GRP)].reshape(192, 128)
            got = mm(split, block, 1, 0).astype(BF16)
            at = pl.ds(pl.multiple_of(b * 96, 96), 96)
            xs[kind, at, 0:128] = got[0:96]
            xs[kind, at, 128:256] = got[96:192]
            return carry

        lax.fori_loop(0, NDP // GRP, unmix, 0)

    def take2(h):
        def unmix(b, carry):
            here = pl.ds(b * GRP, GRP)
            block = jnp.concatenate(
                [frecv2[h, here, 0:3].reshape(192, 128), frecv2[h, here, 3:6].reshape(192, 128)], axis=1
            )
            got = mm(split, block, 1, 0).astype(BF16)
            at = pl.ds(pl.multiple_of(b * 96, 96), 96)
            for j in range(2):
                xs[2 + 2 * h + j, at, 0:128] = got[0:96, 128 * j : 128 * j + 128]
                xs[2 + 2 * h + j, at, 128:256] = got[96:192, 128 * j : 128 * j + 128]
            return carry

        lax.fori_loop(0, NDP // GRP, unmix, 0)

    def give(kind):
        def mix(b, carry):
            at = pl.ds(pl.multiple_of(b * 96, 96), 96)
            v = dq_acc[at, :].astype(BF16)
            got = mm(join, jnp.concatenate([v[:, 0:128], v[:, 128:256]], axis=0), 1, 0).astype(BF16)
            bsend[kind, pl.ds(b * GRP, GRP)] = got.reshape(GRP, 3, 8, 128)
            return carry

        lax.fori_loop(0, NDP // GRP, mix, 0)

    take(1)
    pltpu.make_async_copy(krecv, krecv, kyrecv.at[0]).wait()

    def collect(b, carry):
        at = pl.ds(pl.multiple_of(b * 48, 48), 48)
        got = mm(ctx_out, jnp.concatenate([krecv[t, at, :] for t in range(NY)], axis=0), 1, 0).astype(BF16)
        at = pl.ds(pl.multiple_of(b * 96, 96), 96)
        xs[0, at, 0:128] = got[0:96]
        xs[0, at, 128:256] = got[96:192]
        return carry

    lax.fori_loop(0, NDP // GRP, collect, 0)
    for g in range(2):
        if g == 1:
            for k in range(EARLY):
                spread_out(plane(1 + k), 0, bsend.at[0], brecv.at[0], bsem_s, bsem_r.at[0])
        pltpu.make_async_copy(frecv2.at[g], frecv2.at[g], zrecv.at[2 + g]).wait()
        if g == 1:
            everyone(bsend.at[0], brecv.at[0], bsem_s, bsem_r.at[0], EARLY)
        take2(g)

        def attend(b, carry):
            at = pl.ds(pl.multiple_of(b * HD, HD), HD)
            key, val = xs[0], xs[1]
            qb, gb = xs[2 + 2 * g, at, :], xs[3 + 2 * g, at, :]
            s = mm(key, qb, 1, 1) * SCALE
            ok = labk[:, 0:1] == rowv[0:1, at]
            s = jnp.where(ok, s, MASKED)
            top = jnp.max(s, axis=0, keepdims=True)
            e = jnp.exp(s - top)
            p = e * (1.0 / jnp.sum(e, axis=0, keepdims=True))
            d = mm(val, gb, 1, 1) - rowv[1 + g : 2 + g, at]
            ds = (p * d).astype(BF16)
            pv = mm(p.astype(BF16), gb, 1, 0)
            pk = mm(ds, qb, 1, 0)
            if g == 0:
                first = b == 0
                dv_acc[...] = jnp.where(first, 0.0, dv_acc[...]) + pv
                dk_acc[...] = jnp.where(first, 0.0, dk_acc[...]) + pk
            else:
                dv_acc[...] += pv
                dk_acc[...] += pk
            dq_acc[at, :] = mm(ds, key, 0, 0) * SCALE
            return carry

        if g == 0:
            dv_acc[...] = jnp.zeros((ROWS, HD), F32)
            dk_acc[...] = jnp.zeros((ROWS, HD), F32)
        lax.fori_loop(0, ROWS // HD, attend, 0)
        if g == 0:
            give(0)

    def deal_out(n, acc):
        def deal_back(b, carry):
            at = pl.ds(pl.multiple_of(b * 96, 96), 96)
            v = (acc[at, :] * SCALE if n == 0 else acc[at, :]).astype(BF16)
            got = mm(ctx_in, jnp.concatenate([v[:, 0:128], v[:, 128:256]], axis=0), 1, 0).astype(BF16)
            at = pl.ds(pl.multiple_of(b * 48, 48), 48)
            for t in range(NY):
                dksend[n, t, at, :] = got[48 * t : 48 * t + 48]
            return carry

        lax.fori_loop(0, NDP // GRP, deal_back, 0)
        exchange(dksend.at[n], dkrecv.at[n], kyrecv.at[1 + n])

    deal_out(0, dk_acc)
    give(1)
    everyone(bsend.at[1], brecv.at[1], bsem_s, bsem_r.at[1])
    deal_out(1, dv_acc)

    def home(kind, got, ref, col, sem):
        for t in range(NY):
            obuf[kind, t, :, 0:128] = got[t * TOK : (t + 1) * TOK]
            obuf[kind, t, :, 128:256] = got[(NY + t) * TOK : (NY + t + 1) * TOK]
        cols = pl.ds(pl.multiple_of(col, HD), HD)
        for t in ring_y:
            pltpu.make_async_remote_copy(
                src_ref=obuf.at[kind, t], dst_ref=ref.at[:, cols], send_sem=osem_s, recv_sem=sem,
                device_id=(dp, t), device_id_type=MESH,
            ).start()
        pltpu.make_async_copy(obuf.at[kind, y], ref.at[:, cols], sem).start()

    def home_q(g):
        pltpu.make_async_copy(brecv.at[g], brecv.at[g], bsem_r.at[g]).wait()
        got = mm(gather[...], brecv[g].reshape(2 * ROWS, 128), 1, 0).astype(BF16)
        home(g, got, oq_ref, y * 2 * HD + g * HD, osem_r.at[0])

    for n in range(2):
        pltpu.make_async_copy(dkrecv.at[n], dkrecv.at[n], kyrecv.at[1 + n]).wait()

        def collect_back(b, carry):
            at = pl.ds(pl.multiple_of(b * 48, 48), 48)
            got = mm(head_in, jnp.concatenate([dkrecv[n, t, at, :] for t in range(NY)], axis=0), 1, 0).astype(BF16)
            bsend[2 + n, pl.ds(b * GRP, GRP)] = got.reshape(GRP, 3, 8, 128)
            return carry

        lax.fori_loop(0, NDP // GRP, collect_back, 0)
        by_z(bsend.at[2 + n], brecv.at[2 + n], bsem_s, bsem_r.at[2 + n])
    home_q(0)
    home_q(1)
    for n, ref in enumerate((ok_ref, ov_ref)):
        pltpu.make_async_copy(brecv.at[2 + n], brecv.at[2 + n], bsem_r.at[2 + n]).wait()
        got = mm(kgather[...], brecv[2 + n].reshape(2 * ROWS, 128), 1, 0).astype(BF16)
        for cb in range(8):
            kvout[n, :, cb * TOK : (cb + 1) * TOK] = got[cb * TOK : (cb + 1) * TOK]
        pltpu.make_async_copy(kvout.at[n], ref, osem_r.at[1 + n]).start()

    pltpu.make_async_copy(oq_ref, oq_ref, osem_r.at[0]).wait()
    pltpu.make_async_copy(ok_ref, ok_ref, osem_r.at[1]).wait()
    pltpu.make_async_copy(ov_ref, ov_ref, osem_r.at[2]).wait()
    some = pl.ds(0, NY - 1)
    pltpu.make_async_copy(meta_r.at[some], meta_r.at[some], ymsend).wait()
    pltpu.make_async_copy(del_r.at[some], del_r.at[some], ydsend).wait()
    pltpu.make_async_copy(tok.at[1:NT, some], tok.at[1:NT, some], ysend).wait()
    pltpu.make_async_copy(ksend.at[some], ksend.at[some], kysend).wait()
    pltpu.make_async_copy(dksend.at[:, some], dksend.at[:, some], kysend).wait()
    pltpu.make_async_copy(obuf.at[:, some], obuf.at[:, some], osem_s).wait()
    most = pl.ds(0, NDP - 1)
    pltpu.make_async_copy(msend.at[most], msend.at[most], zmsend).wait()
    pltpu.make_async_copy(fsend.at[:, most], fsend.at[:, most], zsend).wait()
    pltpu.make_async_copy(fsend2.at[:, most], fsend2.at[:, most], zsend).wait()
    pltpu.make_async_copy(bsend.at[:, most], bsend.at[:, most], bsem_s).wait()


def settle(a_ref, b_ref, c_ref, oa_ref, ob_ref, oc_ref, va, vb, vc, sin, sout):
    ways = ((a_ref, va, oa_ref), (b_ref, vb, ob_ref), (c_ref, vc, oc_ref))
    come = [pltpu.make_async_copy(src, mid, sin.at[n]) for n, (src, mid, _) in enumerate(ways)]
    go = [pltpu.make_async_copy(mid, dst, sout.at[n]) for n, (_, mid, dst) in enumerate(ways)]
    for copy in come:
        copy.start()
    for n in range(3):
        come[n].wait()
        go[n].start()
    for copy in go:
        copy.wait()


def body(queries, key_rows, values, saved_out, out_grad, pack_of, segment_label):
    anywhere = pl.BlockSpec(memory_space=pl.ANY)
    hbm = pl.BlockSpec(memory_space=pltpu.HBM)
    dma = pltpu.SemaphoreType.DMA
    shapes = tuple(jax.ShapeDtypeStruct((TOK, n * HD), BF16) for n in (8, 4, 4))
    grads = pl.pallas_call(
        kernel,
        out_shape=shapes,
        in_specs=[hbm] * 7,
        out_specs=(anywhere,) * 3,
        scratch_shapes=[
            pltpu.VMEM((2, 1, TOK), jnp.int32),
            pltpu.VMEM((TOK, 8 * HD), BF16),
            pltpu.VMEM((TOK, 8 * HD), BF16),
            pltpu.VMEM((NT, NY, TOK, HD), BF16),
            pltpu.VMEM((8, TOK), F32),
            pltpu.VMEM((NY, 8, TOK), F32),
            pltpu.VMEM((NY, 8, TOK), F32),
            pltpu.VMEM((NY, 8, TOK), F32),
            pltpu.VMEM((2 * ROWS, 2 * NY * TOK), BF16),
            pltpu.VMEM((2 * NY * TOK, 2 * ROWS), BF16),
            pltpu.VMEM((2, NDP, 3, 8, 128), BF16),
            pltpu.VMEM((2, NDP, 3, 8, 128), BF16),
            pltpu.VMEM((NDP, 1, 128), F32),
            pltpu.VMEM((NDP, 1, 128), F32),
            pltpu.VMEM((NT, ROWS, HD), BF16),
            pltpu.VMEM((8, ROWS), F32),
            pltpu.VMEM((ROWS, 128), F32),
            pltpu.VMEM((ROWS, HD), F32),
            pltpu.VMEM((ROWS, HD), F32),
            pltpu.VMEM((ROWS, HD), F32),
            pltpu.VMEM((4, NDP, 3, 8, 128), BF16),
            pltpu.VMEM((4, NDP, 3, 8, 128), BF16),
            pltpu.VMEM((2, NY, TOK, HD), BF16),
            pltpu.VMEM((2, NDP, 6, 8, 128), BF16),
            pltpu.VMEM((2, NDP, 6, 8, 128), BF16),
            pltpu.VMEM((2, TOK, 4 * HD), BF16),
            pltpu.VMEM((TOK, 4 * HD), BF16),
            pltpu.VMEM((8 * TOK, 2 * ROWS), BF16),
            pltpu.VMEM((NY, 2 * 192, 128), BF16),
            pltpu.VMEM((NY, 2 * 192, 128), BF16),
            pltpu.VMEM((2, NY, 2 * 192, 128), BF16),
            pltpu.VMEM((2, NY, 2 * 192, 128), BF16),
            dma, dma, dma((3,)), dma((2,)), dma((2,)), dma, dma((NT,)), dma, dma, dma, dma, dma, dma((4,)), dma, dma,
            dma, dma((4,)), dma, dma((3,)),
            pltpu.SemaphoreType.REGULAR, pltpu.SemaphoreType.REGULAR,
        ],
        compiler_params=pltpu.CompilerParams(
            collective_id=0, has_side_effects=True, vmem_limit_bytes=63 << 20
        ),
        name="packed_attention_backward",
    )(
        queries, key_rows, values, out_grad, saved_out,
        pack_of.reshape(1, TOK), segment_label.reshape(1, TOK),
    )
    return pl.pallas_call(
        settle,
        out_shape=shapes,
        in_specs=[anywhere] * 3,
        out_specs=(anywhere,) * 3,
        scratch_shapes=[pltpu.VMEM(shape.shape, BF16) for shape in shapes] + [dma((3,)), dma((3,))],
        name="settle",
    )(*grads)


def solution(mesh):
    rows = P(("dp", "ctx"), None)
    return jax.shard_map(
        body,
        mesh=mesh,
        in_specs=(rows, rows, rows, rows, rows, rows, P(("dp", "ctx"))),
        out_specs=(rows, rows, rows),
        check_vma=False,
    )
```
